128 devices in a mesh: aux: 4 (over x), pair: 32 (over z, y, core).
Axes of the slice: x: 4, y: 4, z: 4, core: 2. Of those that a mesh axis runs over, the one named last changes fastest.
Arguments:
- three_index: bfloat16 [512, 256, 2048], P('pair', None, 'aux'), may hold values from -0.875 to 0.875
- fock_diag: float32 [512], replicated, may hold values from -1.2 to -0.3
- pair_occ: int32 [992, 2], P('pair'), may hold values from 0 to 511, as said below
- pno_count: int32 [992], P('pair'), may hold values from 32 to 128
- pno_energy: float32 [992, 128], P('pair'), may hold values from 0.3 to 3
- pno_coef: bfloat16 [992, 2, 256, 128], P('pair'), may hold values from -0.375 to 0.375
Outputs:
- pair_energy: float32 [992], P('pair')
- grad_ints: float32 [512, 256, 2048], P('pair', None, 'aux')
The draws below stay inside these ranges and needn't reach their ends.
Inputs may be any that keep to these rules, and one draw needn't show every extreme that they name: `pair_occ`: orbital o belongs to the block o // 16. Among the 62 orbitals named by the pairs of one aligned block of 31 rows, at most 2 belong to any one orbital block, and one orbital block receives exactly 2 from every such row block; i may equal j.
All inputs are finite; a program needn't handle non-finite values.
Results may differ from the reference program's by a relative error of at most 0.0061.
Values may be sent and summed in bfloat16 or wider, within the bound.
A program may use at most 128 MiB of HBM per device.

```python
import math
import jax
import jax.numpy as jnp
from jax import lax

NDOM = 256
NPNO = 128
NAUXD = 2048
OCC_DEV = 16
PAIR_DEV = 31
OCC = 512
PAIRS = 992
CAP = 2


def draw_pair_occ(key, part):
    groups = PAIRS // PAIR_DEV
    special_key, rest_key = jax.random.split(key)
    special = jax.random.randint(special_key, (), 0, groups)
    owners_all = jnp.arange(groups * CAP, dtype=jnp.int32) // CAP

    def one_block(block_key):
        first_key, second_key, third_key = jax.random.split(block_key, 3)
        scores = jax.random.permutation(first_key, groups * CAP).astype(jnp.int32)
        scores = jnp.where(owners_all == special, scores - groups * CAP, scores)
        order = jnp.argsort(scores, stable=True)
        chosen = owners_all[order][:2 * PAIR_DEV]
        chosen = chosen[jax.random.permutation(second_key, 2 * PAIR_DEV)]
        within = jax.random.randint(third_key, (2 * PAIR_DEV,), 0, OCC_DEV)
        return (chosen * OCC_DEV + within).reshape(PAIR_DEV, 2)
    block_keys = jax.random.split(rest_key, groups)
    return jax.vmap(one_block)(block_keys).reshape(PAIRS, 2).astype(jnp.int32)


def plant(entries, stream_key, least, high):
    shape = entries.shape
    place = [jax.random.randint(jax.random.fold_in(stream_key, axis), (), 0, shape[axis]) for axis in range(len(shape))]
    entries = entries.at[tuple(place)].set(least)
    longest = shape.index(max(shape))
    place[longest] = (place[longest] + 1) % shape[longest]
    return entries.at[tuple(place)].set(high)


def level_of(rng, extent, cuts, smallest, largest):
    def one(position, blocks):
        draws = jax.random.uniform(jax.random.fold_in(jax.random.fold_in(rng, 6), position), (blocks,), jnp.float32, smallest / len(cuts), largest / len(cuts))
        return jnp.repeat(jnp.exp(draws), extent[position] // blocks).reshape((-1,) + (1,) * (len(extent) - position - 1))

    level = one(*cuts[0])
    for cut in cuts[1:]:
        level = level * one(*cut)
    return level


def gaussian(key, shape, spread, limit, cuts=(), held_as=jnp.bfloat16):
    result = jax.random.normal(key, shape, jnp.float32) * spread
    if len(cuts) > 0:
        result = level_of(key, shape, cuts, -0.22, 0.18) * result
    return jnp.clip(result, min=-limit, max=limit).astype(held_as)


def setup_inputs(seed: int = 0) -> dict:
    keys = jax.random.split(jax.random.key(seed), 7)
    three_index = gaussian(keys[0], (OCC, NDOM, NAUXD), (NAUXD ** -0.25), 0.875, ((0, 32), (2, 4)))
    fock_diag = jnp.clip(jax.random.uniform(keys[1], (OCC,), jnp.float32, -1.2, -0.3), -1.2, -0.3)
    pair_occ = draw_pair_occ(jax.random.fold_in(keys[6], 71), 0)
    pno_count = plant(jax.random.randint(keys[3], (PAIRS,), NPNO // 4, NPNO + 1), jax.random.fold_in(keys[3], 1), NPNO // 4, NPNO).astype(jnp.int32)
    pno_energy = jnp.clip(jnp.exp(math.log(3.0) - 2.3025851 * jax.random.uniform(keys[4], (PAIRS, NPNO), jnp.float32) ** level_of(keys[4], (PAIRS, NPNO), ((0, 32),), -0.2, 0.2)), 0.3, 3.0)
    pno_coef = gaussian(keys[5], (PAIRS, 2, NDOM, NPNO), NDOM ** -0.5, 0.375, ((0, 32),))
    return {"three_index": three_index, "fock_diag": fock_diag, "pair_occ": pair_occ, "pno_count": pno_count, "pno_energy": pno_energy, "pno_coef": pno_coef}


def reference(three_index, fock_diag, pair_occ, pno_count, pno_energy, pno_coef):
    in_range = jnp.arange(NPNO, dtype=jnp.int32)

    def add_term(grad, term, occ_row):
        current = lax.dynamic_index_in_dim(grad, occ_row, 0, keepdims=False)
        return lax.dynamic_update_index_in_dim(grad, current + term, occ_row, 0)

    def step(k, carry):
        grad, energies = carry
        occ_i = pair_occ[k, 0]
        occ_j = pair_occ[k, 1]
        block_i = lax.dynamic_index_in_dim(three_index, occ_i, 0, keepdims=False)
        block_j = lax.dynamic_index_in_dim(three_index, occ_j, 0, keepdims=False)
        coef = lax.dynamic_index_in_dim(pno_coef, k, 0, keepdims=False)
        rows_i = jnp.dot(coef[0].T, block_i, preferred_element_type=jnp.float32).astype(jnp.bfloat16)
        rows_j = jnp.dot(coef[1].T, block_j, preferred_element_type=jnp.float32).astype(jnp.bfloat16)
        coupling = jnp.dot(rows_i, rows_j.T, preferred_element_type=jnp.float32)
        energy_row = lax.dynamic_index_in_dim(pno_energy, k, 0, keepdims=False)
        denom = energy_row[:, None] + energy_row[None, :] - fock_diag[occ_i] - fock_diag[occ_j]
        in_pno = in_range < pno_count[k]
        amplitude = jnp.where(in_pno[:, None] & in_pno[None, :], -coupling / denom, jnp.float32(0.0))
        mixed = 2.0 * amplitude - amplitude.T
        energy = jnp.sum(coupling * mixed) / (NPNO * NPNO)
        weights = mixed.astype(jnp.bfloat16)
        gamma_i = jnp.dot(weights, rows_j, preferred_element_type=jnp.float32).astype(jnp.bfloat16)
        gamma_j = jnp.dot(weights.T, rows_i, preferred_element_type=jnp.float32).astype(jnp.bfloat16)
        term_i = lax.optimization_barrier(jnp.dot(coef[0], gamma_i, preferred_element_type=jnp.float32).astype(jnp.bfloat16))
        term_j = lax.optimization_barrier(jnp.dot(coef[1], gamma_j, preferred_element_type=jnp.float32).astype(jnp.bfloat16))
        grad = add_term(grad, term_i.astype(jnp.float32), occ_i)
        grad = add_term(grad, term_j.astype(jnp.float32), occ_j)
        energies = energies.at[k].set(energy)
        return grad, energies

    grad = jnp.zeros((OCC, NDOM, NAUXD), jnp.float32)
    energies = jnp.zeros((PAIRS,), jnp.float32)
    grad, energies = lax.fori_loop(0, PAIRS, step, (grad, energies))
    return energies, grad
```

```python
import functools

import jax
import jax.numpy as jnp
from jax import lax
from jax.experimental import pallas as pl
from jax.experimental.pallas import tpu as pltpu
from jax.sharding import PartitionSpec as P

CAPACITY = 2
STEP_SLOTS = 4
VMEM_LIMIT = 48 << 20


def plan_slots(pair_occ, groups, occ_dev):
    occ_flat = pair_occ.reshape(-1)
    halves = occ_flat.shape[0]
    owner = occ_flat // occ_dev
    half_ids = jnp.arange(halves, dtype=jnp.int32)
    earlier = (owner[None, :] == owner[:, None]) & (half_ids[None, :] < half_ids[:, None])
    rank = jnp.sum(earlier.astype(jnp.int32), axis=1)
    slot_of = owner * CAPACITY + rank
    hot = (slot_of[None, :] == jnp.arange(groups * CAPACITY, dtype=jnp.int32)[:, None]).astype(jnp.int32)
    half_of = jnp.sum(hot * (half_ids + 1)[None, :], axis=1) - 1
    request = jnp.sum(hot * (occ_flat % occ_dev + 1)[None, :], axis=1)
    return slot_of, half_of, request


def gather_kernel(half_ref, coef_ref, out_ref, sem):
    slots, rows = out_ref.shape[0], out_ref.shape[1]
    first = pl.multiple_of(lax.axis_index("aux") * rows, rows)

    def copy(s):
        half = jnp.maximum(half_ref[s], 0)
        return pltpu.make_async_copy(coef_ref.at[half, pl.ds(first, rows)], out_ref.at[s], sem)

    @pl.loop(0, slots)
    def _(s):
        copy(s).start()

    @pl.loop(0, slots)
    def _(s):
        copy(s).wait()


def rows_kernel(row_ref, coef_ref, ints_ref, out_ref):
    step = pl.program_id(0)
    for t in range(STEP_SLOTS):
        row = jnp.maximum(row_ref[step * STEP_SLOTS + t] - 1, 0)
        coef = coef_ref[:, t].reshape(-1, coef_ref.shape[-1])
        out_ref[t] = lax.dot_general(
            coef, ints_ref[row], (((0,), (0,)), ((), ())), preferred_element_type=jnp.float32
        ).astype(out_ref.dtype)


def coupling_kernel(slot_ref, rows_ref, out_ref):
    pairs = out_ref.shape[0]

    @pl.loop(0, pairs)
    def _(k):
        out_ref[k] = lax.dot_general(
            rows_ref[slot_ref[2 * k]],
            rows_ref[slot_ref[2 * k + 1]],
            (((1,), (1,)), ((), ())),
            preferred_element_type=jnp.float32,
        )


def gamma_kernel(slot_ref, occ_ref, count_ref, fock_ref, rows_ref, coupling_ref, energy_in_ref, out_ref, energy_ref):
    pairs, width, _ = coupling_ref.shape
    out_ref[...] = jnp.zeros_like(out_ref)
    row_id = lax.broadcasted_iota(jnp.int32, (width, width), 0)
    col_id = lax.broadcasted_iota(jnp.int32, (width, width), 1)

    @pl.loop(0, pairs)
    def _(k):
        slot_i, slot_j = slot_ref[2 * k], slot_ref[2 * k + 1]
        coupling = coupling_ref[k]
        by_col = jnp.broadcast_to(energy_in_ref[pl.ds(k, 1), :], (width, width))
        denom = by_col.T + by_col - fock_ref[occ_ref[2 * k]] - fock_ref[occ_ref[2 * k + 1]]
        inside = (row_id < count_ref[k]) & (col_id < count_ref[k])
        amplitude = jnp.where(inside, -coupling / denom, 0.0)
        mixed = 2.0 * amplitude - amplitude.T
        energy_ref[pl.ds(k, 1), :] = jnp.sum(coupling * mixed, axis=0, keepdims=True)
        weights = mixed.astype(jnp.bfloat16)
        out_ref[slot_i] = jnp.dot(weights, rows_ref[slot_j], preferred_element_type=jnp.float32).astype(out_ref.dtype)
        out_ref[slot_j] = lax.dot_general(
            weights, rows_ref[slot_i], (((0,), (0,)), ((), ())), preferred_element_type=jnp.float32
        ).astype(out_ref.dtype)


def grad_kernel(row_ref, coef_ref, gamma_ref, out_ref):
    step = pl.program_id(0)

    @pl.when(step == 0)
    def _():
        out_ref[...] = jnp.zeros_like(out_ref)

    for t in range(STEP_SLOTS):
        row = row_ref[step * STEP_SLOTS + t]

        @pl.when(row > 0)
        def _(t=t, row=row):
            coef = coef_ref[:, t].reshape(-1, coef_ref.shape[-1])
            term = jnp.dot(coef, gamma_ref[t], preferred_element_type=jnp.float32).astype(jnp.bfloat16)
            out_ref[row - 1] += term.astype(jnp.float32)


def params():
    return pltpu.CompilerParams(vmem_limit_bytes=VMEM_LIMIT)


def local(three_index, fock_diag, pair_occ, pno_count, pno_energy, pno_coef):
    groups = lax.axis_size("pair")
    planes = lax.axis_size("aux")
    occ_dev, width_dom, width_aux = three_index.shape
    pair_dev = pair_occ.shape[0]
    width_pno = pno_coef.shape[3]
    halves = 2 * pair_dev
    slots = groups * CAPACITY
    part = width_dom // planes
    smem = pl.BlockSpec(memory_space=pltpu.SMEM)
    vmem = pl.BlockSpec(memory_space=pltpu.VMEM)
    hbm = pl.BlockSpec(memory_space=pl.ANY)

    slot_of, half_of, request = plan_slots(pair_occ, groups, occ_dev)

    def exchange(x):
        y = x.reshape((groups, CAPACITY) + x.shape[1:])
        return lax.all_to_all(y, "pair", split_axis=0, concat_axis=0, tiled=True).reshape(x.shape)

    wanted = exchange(request)
    coef_part = pl.pallas_call(
        gather_kernel,
        name="gather_coef",
        out_shape=jax.ShapeDtypeStruct((slots, part, width_pno), jnp.bfloat16),
        in_specs=[smem, hbm],
        out_specs=hbm,
        scratch_shapes=[pltpu.SemaphoreType.DMA],
        compiler_params=params(),
    )(half_of, pno_coef.reshape(halves, width_dom, width_pno))
    coef = lax.all_gather(exchange(coef_part), "aux")

    steps = slots // STEP_SLOTS
    coef_spec = pl.BlockSpec((planes, STEP_SLOTS, part, width_pno), lambda s, r: (0, s, 0, 0))
    whole_spec = pl.BlockSpec((occ_dev, width_dom, width_aux), lambda s, r: (0, 0, 0))
    slot_spec = pl.BlockSpec((STEP_SLOTS, width_pno, width_aux), lambda s, r: (s, 0, 0))
    rows_out = pl.pallas_call(
        rows_kernel,
        name="project_rows",
        out_shape=jax.ShapeDtypeStruct((slots, width_pno, width_aux), jnp.bfloat16),
        grid_spec=pltpu.PrefetchScalarGridSpec(
            num_scalar_prefetch=1, grid=(steps,), in_specs=[coef_spec, whole_spec], out_specs=slot_spec
        ),
        compiler_params=params(),
    )(wanted, coef, three_index)
    rows = exchange(rows_out)

    partial_sum = pl.pallas_call(
        coupling_kernel,
        name="coupling_part",
        out_shape=jax.ShapeDtypeStruct((pair_dev, width_pno, width_pno), jnp.float32),
        in_specs=[smem, vmem],
        out_specs=vmem,
        compiler_params=params(),
    )(slot_of, rows)
    coupling = lax.psum(partial_sum, "aux")

    gamma_out, energy_cols = pl.pallas_call(
        gamma_kernel,
        name="weigh_rows",
        out_shape=(
            jax.ShapeDtypeStruct((slots, width_pno, width_aux), jnp.bfloat16),
            jax.ShapeDtypeStruct((pair_dev, width_pno), jnp.float32),
        ),
        in_specs=[smem, smem, smem, smem, vmem, vmem, vmem],
        out_specs=(vmem, vmem),
        compiler_params=params(),
    )(slot_of, pair_occ.reshape(halves), pno_count, fock_diag, rows, coupling, pno_energy)
    energy = jnp.sum(energy_cols, axis=1) / (width_pno * width_pno)
    gamma = exchange(gamma_out)

    grad = pl.pallas_call(
        grad_kernel,
        name="add_terms",
        out_shape=jax.ShapeDtypeStruct((occ_dev, width_dom, width_aux), jnp.float32),
        grid_spec=pltpu.PrefetchScalarGridSpec(
            num_scalar_prefetch=1, grid=(steps,), in_specs=[coef_spec, slot_spec], out_specs=whole_spec
        ),
        compiler_params=params(),
    )(wanted, coef, gamma)
    return energy, grad


def solution(mesh):
    placed = (
        P("pair", None, "aux"),
        P(),
        P("pair", None),
        P("pair"),
        P("pair", None),
        P("pair", None, None, None),
    )
    return jax.shard_map(
        local,
        mesh=mesh,
        in_specs=placed,
        out_specs=(P("pair"), P("pair", None, "aux")),
        check_vma=False,
    )
```

```python
import functools

import jax
import jax.numpy as jnp
from jax import lax
from jax.experimental import pallas as pl
from jax.experimental.pallas import tpu as pltpu
from jax.sharding import PartitionSpec as P

CAPACITY = 2
STEP_SLOTS = 4
MESH = pl.DeviceIdType.MESH
VMEM_LIMIT = 48 << 20


def plan_slots(pair_occ, groups, occ_dev):
    occ_flat = pair_occ.reshape(-1)
    halves = occ_flat.shape[0]
    owner = occ_flat // occ_dev
    half_ids = jnp.arange(halves, dtype=jnp.int32)
    earlier = (owner[None, :] == owner[:, None]) & (half_ids[None, :] < half_ids[:, None])
    rank = jnp.sum(earlier.astype(jnp.int32), axis=1)
    slot_of = owner * CAPACITY + rank
    hot = (slot_of[None, :] == jnp.arange(groups * CAPACITY, dtype=jnp.int32)[:, None]).astype(jnp.int32)
    half_of = jnp.sum(hot * (half_ids + 1)[None, :], axis=1) - 1
    request = jnp.sum(hot * (occ_flat % occ_dev + 1)[None, :], axis=1)
    return slot_of, half_of, request


def gather_kernel(half_ref, coef_ref, out_ref, sem):
    slots, rows = out_ref.shape[0], out_ref.shape[1]
    first = pl.multiple_of(lax.axis_index("aux") * rows, rows)

    def copy(s):
        half = jnp.maximum(half_ref[s], 0)
        return pltpu.make_async_copy(coef_ref.at[half, pl.ds(first, rows)], out_ref.at[s], sem)

    @pl.loop(0, slots)
    def _(s):
        copy(s).start()

    @pl.loop(0, slots)
    def _(s):
        copy(s).wait()


def place():
    me = lax.axis_index("pair")
    return me // 8, lax.rem(me // 2, 4), lax.rem(me, 2)


def device(z, y, core):
    return {"pair": (z * 4 + y) * 2 + core}


def greet():
    z, y, core = place()
    barrier = pltpu.get_barrier_semaphore()
    peers = [device(z, y, 1 - core)]
    for d in (1, 2, 3):
        for c in (core, 1 - core):
            peers += [device(lax.rem(z + d, 4), y, c), device(z, lax.rem(y + d, 4), c)]
    for peer in peers:
        pl.semaphore_signal(barrier, inc=1, device_id=peer, device_id_type=MESH)
    pl.semaphore_wait(barrier, len(peers))


def exchange_in_kernel(produce, send, transit, recv, hop_send, hop_recv, last_send, last_recv):
    z, y, core = place()
    here, across = (z, y), (y, z)
    hops = {}
    for d in (1, 3, 2, 0):
        for way in (0, 1):
            group = lax.rem(here[way] + d, 4)
            produce(way, group)
            if d:
                n = way * 3 + d - 1
                hops[way, d] = pltpu.make_async_remote_copy(
                    src_ref=send.at[way, group],
                    dst_ref=transit.at[way, here[way]],
                    send_sem=hop_send.at[n],
                    recv_sem=hop_recv.at[n],
                    device_id=device(group, y, core) if way == 0 else device(z, group, core),
                    device_id_type=MESH,
                )
                hops[way, d].start()
    last = []
    for ds in (0, 1, 3, 2):
        for way in (0, 1):
            source = lax.rem(here[way] + 4 - ds, 4)
            if ds:
                hops[way, ds].wait_recv()
            origin = (source * 4 + y) * 2 + core if way == 0 else (z * 4 + source) * 2 + core
            for d in (1, 3, 2, 0):
                for dc in (0, 1):
                    to, to_core = lax.rem(across[way] + d, 4), lax.rem(core + dc, 2)
                    block = (transit if ds else send).at[way, source, to * 2 + to_core]
                    n = ((way * 4 + ds) * 4 + d) * 2 + dc
                    if d == 0 and dc == 0:
                        copy = pltpu.make_async_copy(block, recv.at[origin, way], last_send.at[n])
                    else:
                        copy = pltpu.make_async_remote_copy(
                            src_ref=block,
                            dst_ref=recv.at[origin, way],
                            send_sem=last_send.at[n],
                            recv_sem=last_recv.at[n],
                            device_id=device(z, to, to_core) if way == 0 else device(to, y, to_core),
                            device_id_type=MESH,
                        )
                    copy.start()
                    last.append(copy)
    for hop in hops.values():
        hop.wait_send()
    for copy in last:
        copy.wait()


def exchange_scratch(shape):
    return [
        pltpu.VMEM((2, 4, 8) + shape, jnp.bfloat16),
        pltpu.VMEM((2, 4, 8) + shape, jnp.bfloat16),
        pltpu.SemaphoreType.DMA((6,)),
        pltpu.SemaphoreType.DMA((6,)),
        pltpu.SemaphoreType.DMA((64,)),
        pltpu.SemaphoreType.DMA((64,)),
    ]


def rows_kernel(row_ref, coef_ref, ints_ref, recv_ref, send_ref, transit_ref, *sems):
    greet()

    def produce(way, group):
        @pl.loop(0, 8)
        def _(t):
            owner = group * 8 + t if way == 0 else (t // 2 * 4 + group) * 2 + lax.rem(t, 2)
            slot = owner * CAPACITY + way
            coef = coef_ref[:, slot].reshape(-1, coef_ref.shape[-1])
            row = jnp.maximum(row_ref[slot] - 1, 0)
            send_ref[way, group, t] = lax.dot_general(
                coef, ints_ref[row], (((0,), (0,)), ((), ())), preferred_element_type=jnp.float32
            ).astype(send_ref.dtype)

    exchange_in_kernel(produce, send_ref, transit_ref, recv_ref, *sems)


def coupling_kernel(slot_ref, rows_ref, out_ref):
    pairs = out_ref.shape[0]

    @pl.loop(0, pairs)
    def _(k):
        out_ref[k] = lax.dot_general(
            rows_ref[slot_ref[2 * k]],
            rows_ref[slot_ref[2 * k + 1]],
            (((1,), (1,)), ((), ())),
            preferred_element_type=jnp.float32,
        )


def gamma_kernel(slot_ref, occ_ref, count_ref, fock_ref, rows_ref, coupling_ref, energy_in_ref, out_ref, energy_ref):
    pairs, width, _ = coupling_ref.shape
    out_ref[...] = jnp.zeros_like(out_ref)
    row_id = lax.broadcasted_iota(jnp.int32, (width, width), 0)
    col_id = lax.broadcasted_iota(jnp.int32, (width, width), 1)

    @pl.loop(0, pairs)
    def _(k):
        slot_i, slot_j = slot_ref[2 * k], slot_ref[2 * k + 1]
        coupling = coupling_ref[k]
        by_col = jnp.broadcast_to(energy_in_ref[pl.ds(k, 1), :], (width, width))
        denom = by_col.T + by_col - fock_ref[occ_ref[2 * k]] - fock_ref[occ_ref[2 * k + 1]]
        inside = (row_id < count_ref[k]) & (col_id < count_ref[k])
        amplitude = jnp.where(inside, -coupling / denom, 0.0)
        mixed = 2.0 * amplitude - amplitude.T
        energy_ref[pl.ds(k, 1), :] = jnp.sum(coupling * mixed, axis=0, keepdims=True)
        weights = mixed.astype(jnp.bfloat16)
        out_ref[slot_i] = jnp.dot(weights, rows_ref[slot_j], preferred_element_type=jnp.float32).astype(out_ref.dtype)
        out_ref[slot_j] = lax.dot_general(
            weights, rows_ref[slot_i], (((0,), (0,)), ((), ())), preferred_element_type=jnp.float32
        ).astype(out_ref.dtype)


def grad_kernel(row_ref, coef_ref, gamma_ref, out_ref):
    step = pl.program_id(0)

    @pl.when(step == 0)
    def _():
        out_ref[...] = jnp.zeros_like(out_ref)

    for t in range(STEP_SLOTS):
        row = row_ref[step * STEP_SLOTS + t]

        @pl.when(row > 0)
        def _(t=t, row=row):
            coef = coef_ref[:, t].reshape(-1, coef_ref.shape[-1])
            term = jnp.dot(coef, gamma_ref[t], preferred_element_type=jnp.float32).astype(jnp.bfloat16)
            out_ref[row - 1] += term.astype(jnp.float32)


def params(collective_id=None):
    return pltpu.CompilerParams(
        vmem_limit_bytes=VMEM_LIMIT, collective_id=collective_id, has_side_effects=collective_id is not None
    )


def local(three_index, fock_diag, pair_occ, pno_count, pno_energy, pno_coef):
    groups = lax.axis_size("pair")
    planes = lax.axis_size("aux")
    occ_dev, width_dom, width_aux = three_index.shape
    pair_dev = pair_occ.shape[0]
    width_pno = pno_coef.shape[3]
    halves = 2 * pair_dev
    slots = groups * CAPACITY
    part = width_dom // planes
    smem = pl.BlockSpec(memory_space=pltpu.SMEM)
    vmem = pl.BlockSpec(memory_space=pltpu.VMEM)
    hbm = pl.BlockSpec(memory_space=pl.ANY)

    slot_of, half_of, request = plan_slots(pair_occ, groups, occ_dev)

    def exchange(x):
        y = x.reshape((groups, CAPACITY) + x.shape[1:])
        return lax.all_to_all(y, "pair", split_axis=0, concat_axis=0, tiled=True).reshape(x.shape)

    wanted = exchange(request)
    coef_part = pl.pallas_call(
        gather_kernel,
        name="gather_coef",
        out_shape=jax.ShapeDtypeStruct((slots, part, width_pno), jnp.bfloat16),
        in_specs=[smem, hbm],
        out_specs=hbm,
        scratch_shapes=[pltpu.SemaphoreType.DMA],
        compiler_params=params(),
    )(half_of, pno_coef.reshape(halves, width_dom, width_pno))
    coef = lax.all_gather(exchange(coef_part), "aux")

    steps = slots // STEP_SLOTS
    coef_spec = pl.BlockSpec((planes, STEP_SLOTS, part, width_pno), lambda s, r: (0, s, 0, 0))
    whole_spec = pl.BlockSpec((occ_dev, width_dom, width_aux), lambda s, r: (0, 0, 0))
    slot_spec = pl.BlockSpec((STEP_SLOTS, width_pno, width_aux), lambda s, r: (s, 0, 0))
    rows = pl.pallas_call(
        rows_kernel,
        name="project_and_return_rows",
        out_shape=jax.ShapeDtypeStruct((groups, CAPACITY, width_pno, width_aux), jnp.bfloat16),
        in_specs=[smem, vmem, vmem],
        out_specs=hbm,
        scratch_shapes=exchange_scratch((width_pno, width_aux)),
        compiler_params=params(1),
    )(wanted, coef, three_index).reshape(slots, width_pno, width_aux)

    partial_sum = pl.pallas_call(
        coupling_kernel,
        name="coupling_part",
        out_shape=jax.ShapeDtypeStruct((pair_dev, width_pno, width_pno), jnp.float32),
        in_specs=[smem, vmem],
        out_specs=vmem,
        compiler_params=params(),
    )(slot_of, rows)
    coupling = lax.psum(partial_sum, "aux")

    gamma_out, energy_cols = pl.pallas_call(
        gamma_kernel,
        name="weigh_rows",
        out_shape=(
            jax.ShapeDtypeStruct((slots, width_pno, width_aux), jnp.bfloat16),
            jax.ShapeDtypeStruct((pair_dev, width_pno), jnp.float32),
        ),
        in_specs=[smem, smem, smem, smem, vmem, vmem, vmem],
        out_specs=(vmem, vmem),
        compiler_params=params(),
    )(slot_of, pair_occ.reshape(halves), pno_count, fock_diag, rows, coupling, pno_energy)
    energy = jnp.sum(energy_cols, axis=1) / (width_pno * width_pno)
    gamma = exchange(gamma_out)

    grad = pl.pallas_call(
        grad_kernel,
        name="add_terms",
        out_shape=jax.ShapeDtypeStruct((occ_dev, width_dom, width_aux), jnp.float32),
        grid_spec=pltpu.PrefetchScalarGridSpec(
            num_scalar_prefetch=1, grid=(steps,), in_specs=[coef_spec, slot_spec], out_specs=whole_spec
        ),
        compiler_params=params(),
    )(wanted, coef, gamma)
    return energy, grad


def solution(mesh):
    placed = (
        P("pair", None, "aux"),
        P(),
        P("pair", None),
        P("pair"),
        P("pair", None),
        P("pair", None, None, None),
    )
    return jax.shard_map(
        local,
        mesh=mesh,
        in_specs=placed,
        out_specs=(P("pair"), P("pair", None, "aux")),
        check_vma=False,
    )
```

```python
import functools

import jax
import jax.numpy as jnp
from jax import lax
from jax.experimental import pallas as pl
from jax.experimental.pallas import tpu as pltpu
from jax.sharding import PartitionSpec as P

CAPACITY = 2
MESH = pl.DeviceIdType.MESH
GROUP_ORDER = (1, 3, 2, 0)
VMEM_LIMIT = 48 << 20


def plan_slots(pair_occ, groups, occ_dev):
    occ_flat = pair_occ.reshape(-1)
    halves = occ_flat.shape[0]
    owner = occ_flat // occ_dev
    half_ids = jnp.arange(halves, dtype=jnp.int32)
    earlier = (owner[None, :] == owner[:, None]) & (half_ids[None, :] < half_ids[:, None])
    rank = jnp.sum(earlier.astype(jnp.int32), axis=1)
    slot_of = owner * CAPACITY + rank
    hot = (slot_of[None, :] == jnp.arange(groups * CAPACITY, dtype=jnp.int32)[:, None]).astype(jnp.int32)
    half_of = jnp.sum(hot * (half_ids + 1)[None, :], axis=1) - 1
    request = jnp.sum(hot * (occ_flat % occ_dev + 1)[None, :], axis=1)
    partner = jnp.sum(hot * slot_of.reshape(-1, 2)[:, ::-1].reshape(-1)[None, :], axis=1)
    return slot_of, half_of, request, partner


def place():
    me = lax.axis_index("pair")
    return me // 8, lax.rem(me // 2, 4), lax.rem(me, 2)


def device(z, y, core):
    return {"pair": (z * 4 + y) * 2 + core}


def plane(d):
    return {"aux": lax.rem(lax.axis_index("aux") + d, 4)}


def greet():
    z, y, core = place()
    barrier = pltpu.get_barrier_semaphore()
    peers = [device(z, y, 1 - core)]
    for d in (1, 2, 3):
        peers.append(plane(d))
        for c in (core, 1 - core):
            peers += [device(lax.rem(z + d, 4), y, c), device(z, lax.rem(y + d, 4), c)]
    for peer in peers:
        pl.semaphore_signal(barrier, inc=1, device_id=peer, device_id_type=MESH)
    pl.semaphore_wait(barrier, len(peers))


def start_exchange(produce, deliver, send, transit, hop_send, hop_recv, last_send, last_recv):
    z, y, core = place()
    here, across = (z, y), (y, z)
    hops, last = {}, {}
    for d in GROUP_ORDER:
        for way in (0, 1):
            group = lax.rem(here[way] + d, 4)
            produce(way, d, group)
            if d:
                n = way * 3 + d - 1
                hops[way, d] = pltpu.make_async_remote_copy(
                    src_ref=send.at[way, group],
                    dst_ref=transit.at[way, here[way]],
                    send_sem=hop_send.at[n],
                    recv_sem=hop_recv.at[n],
                    device_id=device(group, y, core) if way == 0 else device(z, group, core),
                    device_id_type=MESH,
                )
                hops[way, d].start()
    for ds in (0, 1, 3, 2):
        for way in (0, 1):
            source = lax.rem(here[way] + 4 - ds, 4)
            if ds:
                hops[way, ds].wait_recv()
            last[way, ds] = []
            for d in GROUP_ORDER:
                for dc in (0, 1):
                    to, to_core = lax.rem(across[way] + d, 4), lax.rem(core + dc, 2)
                    block = (transit if ds else send).at[way, source, to * 2 + to_core]
                    dst = deliver(way, source, across[way] * 2 + core)
                    n = ((way * 4 + ds) * 4 + d) * 2 + dc
                    if d == 0 and dc == 0:
                        copy = pltpu.make_async_copy(block, dst, last_send.at[n])
                    else:
                        copy = pltpu.make_async_remote_copy(
                            src_ref=block,
                            dst_ref=dst,
                            send_sem=last_send.at[n],
                            recv_sem=last_recv.at[n],
                            device_id=device(z, to, to_core) if way == 0 else device(to, y, to_core),
                            device_id_type=MESH,
                        )
                    copy.start()
                    last[way, ds].append((copy, d > 0 or dc > 0))
    return hops, last


def wait_arrivals(copies):
    for copy, remote in copies:
        if remote:
            copy.wait_recv()
        else:
            copy.wait()


def wait_sends(hops, last):
    for hop in hops.values():
        hop.wait_send()
    for copies in last.values():
        for copy, remote in copies:
            if remote:
                copy.wait_send()


def exchange_in_kernel(produce, deliver, *scratch):
    hops, last = start_exchange(produce, deliver, *scratch)
    for copies in last.values():
        wait_arrivals(copies)
    wait_sends(hops, last)


def exchange_scratch(shape):
    return [
        pltpu.VMEM((2, 4, 8) + shape, jnp.bfloat16),
        pltpu.VMEM((2, 4, 8) + shape, jnp.bfloat16),
        pltpu.SemaphoreType.DMA((6,)),
        pltpu.SemaphoreType.DMA((6,)),
        pltpu.SemaphoreType.DMA((64,)),
        pltpu.SemaphoreType.DMA((64,)),
    ]


def slot_at(way, group, t):
    owner = group * 8 + t if way == 0 else (t // 2 * 4 + group) * 2 + lax.rem(t, 2)
    return owner * CAPACITY + way


def start_tables(table, hop_send, hop_recv, last_send, last_recv):
    z, y, core = place()
    mine = y * 2 + core
    hops, last = [], []
    for d in (1, 3, 2):
        hops.append(
            pltpu.make_async_remote_copy(
                src_ref=table.at[mine, z],
                dst_ref=table.at[mine, z],
                send_sem=hop_send.at[d - 1],
                recv_sem=hop_recv.at[d - 1],
                device_id=device(lax.rem(z + d, 4), y, core),
                device_id_type=MESH,
            )
        )
        hops[-1].start()
    for copy in hops:
        copy.wait()
    for d in GROUP_ORDER:
        for dc in (0, 1):
            if d or dc:
                n = d * 2 + dc
                last.append(
                    pltpu.make_async_remote_copy(
                        src_ref=table.at[mine],
                        dst_ref=table.at[mine],
                        send_sem=last_send.at[n],
                        recv_sem=last_recv.at[n],
                        device_id=device(z, lax.rem(y + d, 4), lax.rem(core + dc, 2)),
                        device_id_type=MESH,
                    )
                )
                last[-1].start()
    return last


def fetch_kernel(
    half_ref, request_ref, own_coef_ref, ints_hbm_ref,
    recv_ref, coef_ref, wanted_ref,
    ints_ref, ints_sem, table_ref, table_smem, table_sem,
    table_hop_send, table_hop_recv, table_last_send, table_last_recv,
    coef_send_ref, coef_transit_ref, coef_hop_send, coef_hop_recv, coef_last_send, coef_last_recv,
    plane_send, plane_recv,
    send_ref, transit_ref, *sems,
):
    z, y, core = place()
    here = (z, y)
    mine = lax.axis_index("aux")
    rows = coef_ref.shape[4]
    first = pl.multiple_of(mine * rows, rows)
    load = pltpu.make_async_copy(ints_hbm_ref, ints_ref, ints_sem)
    load.start()
    table_ref[y * 2 + core, z] = request_ref[...]
    greet()

    def pick(way, d, group):
        @pl.loop(0, 8)
        def _(t):
            coef_send_ref[way, group, t] = own_coef_ref[half_ref[slot_at(way, group, t)], pl.ds(first, rows), :]

    coef_hops, coef_last = start_exchange(
        pick,
        lambda way, group, t: coef_ref.at[mine, way, group, t],
        coef_send_ref, coef_transit_ref, coef_hop_send, coef_hop_recv, coef_last_send, coef_last_recv,
    )
    tables = start_tables(table_ref, table_hop_send, table_hop_recv, table_last_send, table_last_recv)

    batches = [(way, (4 - d) % 4) for d in GROUP_ORDER for way in (0, 1)]
    shared = {}

    def share(way, ds):
        wait_arrivals(coef_last[way, ds])
        block = coef_ref.at[mine, way, lax.rem(here[way] + 4 - ds, 4)]
        shared[way, ds] = []
        for d in (2, 1, 3):
            n = (way * 4 + ds) * 3 + d - 1
            copy = pltpu.make_async_remote_copy(
                src_ref=block,
                dst_ref=block,
                send_sem=plane_send.at[n],
                recv_sem=plane_recv.at[n],
                device_id=plane(d),
                device_id_type=MESH,
            )
            copy.start()
            shared[way, ds].append(copy)

    for batch in batches[:2]:
        share(*batch)
    for copy in tables:
        copy.wait()
    to_smem = pltpu.make_async_copy(table_ref, table_smem, table_sem)
    to_smem.start()
    to_smem.wait()
    load.wait()
    me = lax.axis_index("pair")

    def produce(way, d, group):
        place_in_order = batches.index((way, (4 - d) % 4))
        if place_in_order + 2 < len(batches):
            share(*batches[place_in_order + 2])
        for copy in shared[way, (4 - d) % 4]:
            copy.wait_recv()

        @pl.loop(0, 8)
        def _(t):
            slot = slot_at(way, group, t)
            owner = slot // CAPACITY
            wanted = table_smem[lax.rem(owner, 8), owner // 8, 0, me * CAPACITY + way]
            wanted_ref[slot] = wanted
            coef = coef_ref[:, way, group, t].reshape(-1, coef_ref.shape[-1])
            send_ref[way, group, t] = lax.dot_general(
                coef, ints_ref[jnp.maximum(wanted - 1, 0)], (((0,), (0,)), ((), ())),
                preferred_element_type=jnp.float32,
            ).astype(send_ref.dtype)

    exchange_in_kernel(
        produce,
        lambda way, group, t: recv_ref.at[group * 8 + t if way == 0 else (t // 2 * 4 + group) * 2 + lax.rem(t, 2), way],
        send_ref, transit_ref, *sems,
    )
    wait_sends(coef_hops, coef_last)
    for copies in shared.values():
        for copy in copies:
            copy.wait_send()


def couple_kernel(
    slot_ref, pair_ref, side_ref, partner_ref, occ_ref, count_ref, fock_ref, energy_in_ref, rows_ref,
    recv_ref, energy_ref,
    part_ref, inbox_ref, weights_ref, sum_send, sum_recv, weight_send, weight_recv, energy_send, energy_recv,
    send_ref, transit_ref, *sems,
):
    share, width = part_ref.shape[1], part_ref.shape[2]
    pairs = count_ref.shape[0]
    mine = lax.axis_index("aux")
    greet()

    def part(d):
        first = lax.rem(mine + d, 4) * share

        @pl.loop(0, share)
        def _(t):
            k = jnp.minimum(first + t, pairs - 1)
            part_ref[d, t] = lax.dot_general(
                rows_ref[slot_ref[2 * k]],
                rows_ref[slot_ref[2 * k + 1]],
                (((1,), (1,)), ((), ())),
                preferred_element_type=jnp.float32,
            )

    sums = []
    for d in (2, 1, 3):
        part(d)
        sums.append(
            pltpu.make_async_remote_copy(
                src_ref=part_ref.at[d],
                dst_ref=inbox_ref.at[d - 1],
                send_sem=sum_send.at[d - 1],
                recv_sem=sum_recv.at[d - 1],
                device_id=plane(d),
                device_id_type=MESH,
            )
        )
        sums[-1].start()
    part(0)
    for copy in sums:
        copy.wait()

    row_id = lax.broadcasted_iota(jnp.int32, (width, width), 0)
    col_id = lax.broadcasted_iota(jnp.int32, (width, width), 1)

    @pl.loop(0, share)
    def _(t):
        k = jnp.minimum(mine * share + t, pairs - 1)
        coupling = (part_ref[0, t] + inbox_ref[0, t]) + (inbox_ref[1, t] + inbox_ref[2, t])
        by_col = jnp.broadcast_to(energy_in_ref[pl.ds(k, 1), :], (width, width))
        denom = by_col.T + by_col - fock_ref[occ_ref[2 * k]] - fock_ref[occ_ref[2 * k + 1]]
        inside = (row_id < count_ref[k]) & (col_id < count_ref[k])
        amplitude = jnp.where(inside, -coupling / denom, 0.0)
        mixed = 2.0 * amplitude - amplitude.T
        energy_ref[mine, pl.ds(t, 1), :] = jnp.sum(coupling * mixed, axis=0, keepdims=True)
        weights_ref[mine, t] = mixed.astype(jnp.bfloat16)

    copies = []
    for d in (2, 1, 3):
        for ref, out, got in ((weights_ref, weight_send, weight_recv), (energy_ref, energy_send, energy_recv)):
            copies.append(
                pltpu.make_async_remote_copy(
                    src_ref=ref.at[mine],
                    dst_ref=ref.at[mine],
                    send_sem=out.at[d - 1],
                    recv_sem=got.at[d - 1],
                    device_id=plane(d),
                    device_id_type=MESH,
                )
            )
            copies[-1].start()
    for copy in copies:
        copy.wait()

    def produce(way, d, group):
        @pl.loop(0, 8)
        def _(t):
            slot = slot_at(way, group, t)
            pair = pair_ref[slot]
            weights = weights_ref[pair // share, lax.rem(pair, share)].astype(jnp.float32)
            weights = jnp.where(side_ref[slot] == 0, weights, weights.T).astype(jnp.bfloat16)
            send_ref[way, group, t] = jnp.dot(
                weights, rows_ref[partner_ref[slot]], preferred_element_type=jnp.float32
            ).astype(send_ref.dtype)

    exchange_in_kernel(
        produce, lambda way, group, t: recv_ref.at[way, group, t], send_ref, transit_ref, *sems
    )


def grad_kernel(wanted_ref, coef_ref, gamma_ref, out_ref):
    step = pl.program_id(0)

    @pl.when(step == 0)
    def _():
        out_ref[...] = jnp.zeros_like(out_ref)

    for t in range(8):
        wanted = wanted_ref[slot_at_step(step, t)]

        @pl.when(wanted > 0)
        def _(t=t, wanted=wanted):
            coef = coef_ref[:, 0, 0, t].reshape(-1, coef_ref.shape[-1])
            term = jnp.dot(coef, gamma_ref[0, 0, t], preferred_element_type=jnp.float32).astype(jnp.bfloat16)
            out_ref[wanted - 1] += term.astype(jnp.float32)


def slot_at_step(step, t):
    group = lax.rem(step, 4)
    return jnp.where(step < 4, slot_at(0, group, t), slot_at(1, group, t))


def params(collective_id=None):
    return pltpu.CompilerParams(
        vmem_limit_bytes=VMEM_LIMIT, collective_id=collective_id, has_side_effects=collective_id is not None
    )


def local(three_index, fock_diag, pair_occ, pno_count, pno_energy, pno_coef):
    groups = lax.axis_size("pair")
    planes = lax.axis_size("aux")
    occ_dev, width_dom, width_aux = three_index.shape
    pair_dev = pair_occ.shape[0]
    width_pno = pno_coef.shape[3]
    halves = 2 * pair_dev
    slots = groups * CAPACITY
    part = width_dom // planes
    smem = pl.BlockSpec(memory_space=pltpu.SMEM)
    vmem = pl.BlockSpec(memory_space=pltpu.VMEM)
    hbm = pl.BlockSpec(memory_space=pl.ANY)

    slot_of, half_of, request, partner = plan_slots(pair_occ, groups, occ_dev)

    half = jnp.maximum(half_of, 0)
    coef_block = (part, width_pno)
    rows, coef, wanted = pl.pallas_call(
        fetch_kernel,
        name="fetch_coef_and_return_rows",
        out_shape=(
            jax.ShapeDtypeStruct((groups, CAPACITY, width_pno, width_aux), jnp.bfloat16),
            jax.ShapeDtypeStruct((planes, CAPACITY, 4, 8, part, width_pno), jnp.bfloat16),
            jax.ShapeDtypeStruct((slots,), jnp.int32),
        ),
        in_specs=[smem, vmem, vmem, hbm],
        out_specs=(hbm, vmem, smem),
        scratch_shapes=[
            pltpu.VMEM((occ_dev, width_dom, width_aux), jnp.bfloat16),
            pltpu.SemaphoreType.DMA,
            pltpu.VMEM((8, 4, 8, 128), jnp.int32),
            pltpu.SMEM((8, 4, 8, 128), jnp.int32),
            pltpu.SemaphoreType.DMA,
            pltpu.SemaphoreType.DMA((3,)),
            pltpu.SemaphoreType.DMA((3,)),
            pltpu.SemaphoreType.DMA((8,)),
            pltpu.SemaphoreType.DMA((8,)),
        ]
        + exchange_scratch(coef_block)
        + [pltpu.SemaphoreType.DMA((24,)), pltpu.SemaphoreType.DMA((24,))]
        + exchange_scratch((width_pno, width_aux)),
        compiler_params=params(1),
    )(
        half,
        jnp.pad(request[None, :], ((0, 7), (0, 128 - slots))),
        pno_coef.reshape(halves, width_dom, width_pno),
        three_index,
    )
    rows = rows.reshape(slots, width_pno, width_aux)

    share = -(-pair_dev // planes)
    gamma, energy_cols = pl.pallas_call(
        couple_kernel,
        name="couple_and_return_gamma",
        out_shape=(
            jax.ShapeDtypeStruct((CAPACITY, 4, 8, width_pno, width_aux), jnp.bfloat16),
            jax.ShapeDtypeStruct((planes, share, width_pno), jnp.float32),
        ),
        in_specs=[smem] * 7 + [vmem] * 2,
        out_specs=(hbm, vmem),
        scratch_shapes=[
            pltpu.VMEM((planes, share, width_pno, width_pno), jnp.float32),
            pltpu.VMEM((planes - 1, share, width_pno, width_pno), jnp.float32),
            pltpu.VMEM((planes, share, width_pno, width_pno), jnp.bfloat16),
        ]
        + [pltpu.SemaphoreType.DMA((planes - 1,))] * 6
        + exchange_scratch((width_pno, width_aux)),
        compiler_params=params(2),
    )(slot_of, half // 2, half % 2, partner, pair_occ.reshape(halves), pno_count, fock_diag, pno_energy, rows)
    energy = jnp.sum(energy_cols, axis=2).reshape(-1)[:pair_dev] / (width_pno * width_pno)
    grad = pl.pallas_call(
        grad_kernel,
        name="add_terms",
        out_shape=jax.ShapeDtypeStruct((occ_dev, width_dom, width_aux), jnp.float32),
        grid_spec=pltpu.PrefetchScalarGridSpec(
            num_scalar_prefetch=1,
            grid=(8,),
            in_specs=[
                pl.BlockSpec((planes, 1, 1, 8, part, width_pno), lambda s, w: (0, s // 4, s % 4, 0, 0, 0)),
                pl.BlockSpec((1, 1, 8, width_pno, width_aux), lambda s, w: (s // 4, s % 4, 0, 0, 0)),
            ],
            out_specs=pl.BlockSpec((occ_dev, width_dom, width_aux), lambda s, w: (0, 0, 0)),
        ),
        compiler_params=params(),
    )(wanted, coef, gamma)
    return energy, grad


def solution(mesh):
    placed = (
        P("pair", None, "aux"),
        P(),
        P("pair", None),
        P("pair"),
        P("pair", None),
        P("pair", None, None, None),
    )
    return jax.shard_map(
        local,
        mesh=mesh,
        in_specs=placed,
        out_specs=(P("pair"), P("pair", None, "aux")),
        check_vma=False,
    )
```

```python
import functools

import jax
import jax.numpy as jnp
from jax import lax
from jax.experimental import pallas as pl
from jax.experimental.pallas import tpu as pltpu
from jax.sharding import PartitionSpec as P

CAPACITY = 2
MESH = pl.DeviceIdType.MESH
GROUP_ORDER = (1, 3, 2, 0)
OWN_FIRST = (0, 1, 3, 2)
SUMMED_IN_PARTS = 2


def plan_slots(pair_occ, groups, occ_dev):
    occ_flat = pair_occ.reshape(-1)
    halves = occ_flat.shape[0]
    owner = occ_flat // occ_dev
    half_ids = jnp.arange(halves, dtype=jnp.int32)
    earlier = (owner[None, :] == owner[:, None]) & (half_ids[None, :] < half_ids[:, None])
    rank = jnp.sum(earlier.astype(jnp.int32), axis=1)
    slot_of = owner * CAPACITY + rank
    hot = (slot_of[None, :] == jnp.arange(groups * CAPACITY, dtype=jnp.int32)[:, None]).astype(jnp.int32)
    half_of = jnp.sum(hot * (half_ids + 1)[None, :], axis=1) - 1
    request = jnp.sum(hot * (occ_flat % occ_dev + 1)[None, :], axis=1)
    partner = jnp.sum(hot * slot_of.reshape(-1, 2)[:, ::-1].reshape(-1)[None, :], axis=1)
    return slot_of, half_of, request, partner


def place():
    me = lax.axis_index("pair")
    return me // 8, lax.rem(me // 2, 4), lax.rem(me, 2)


def device(z, y, core):
    return {"pair": (z * 4 + y) * 2 + core}


def plane(d):
    return {"aux": lax.rem(lax.axis_index("aux") + d, 4)}


def greet():
    z, y, core = place()
    barrier = pltpu.get_barrier_semaphore()
    peers = [device(z, y, 1 - core)]
    for d in (1, 2, 3):
        peers.append(plane(d))
        for c in (core, 1 - core):
            peers += [device(lax.rem(z + d, 4), y, c), device(z, lax.rem(y + d, 4), c)]
    for peer in peers:
        pl.semaphore_signal(barrier, inc=1, device_id=peer, device_id_type=MESH)
    pl.semaphore_wait(barrier, len(peers))


def start_exchange(produce, deliver, order, between, send, transit, hop_send, hop_recv, last_send, last_recv):
    z, y, core = place()
    here, across = (z, y), (y, z)
    hops, last = {}, {}

    def hop(way, d):
        group, n = lax.rem(here[way] + d, 4), way * 3 + d - 1
        hops[way, d] = pltpu.make_async_remote_copy(
            src_ref=send.at[way, group],
            dst_ref=transit.at[way, here[way]],
            send_sem=hop_send.at[n],
            recv_sem=hop_recv.at[n],
            device_id=device(group, y, core) if way == 0 else device(z, group, core),
            device_id_type=MESH,
        )
        hops[way, d].start()

    def spread(way, ds):
        source = lax.rem(here[way] + 4 - ds, 4)
        last[way, ds] = []
        for d in GROUP_ORDER:
            for dc in (0, 1):
                to, to_core = lax.rem(across[way] + d, 4), lax.rem(core + dc, 2)
                block = (transit if ds else send).at[way, source, to * 2 + to_core]
                dst = deliver(way, source, across[way] * 2 + core)
                n = ((way * 4 + ds) * 4 + d) * 2 + dc
                if d == 0 and dc == 0:
                    copy = pltpu.make_async_copy(block, dst, last_send.at[n])
                else:
                    copy = pltpu.make_async_remote_copy(
                        src_ref=block,
                        dst_ref=dst,
                        send_sem=last_send.at[n],
                        recv_sem=last_recv.at[n],
                        device_id=device(z, to, to_core) if way == 0 else device(to, y, to_core),
                        device_id_type=MESH,
                    )
                copy.start()
                last[way, ds].append((copy, d > 0 or dc > 0))

    for d in order:
        for way in (0, 1):
            produce(way, d, lax.rem(here[way] + d, 4))
            if d:
                hop(way, d)
            else:
                spread(way, 0)
    between()
    for ds in (1, 3, 2):
        for way in (0, 1):
            hops[way, ds].wait_recv()
            spread(way, ds)
    return hops, last


def wait_arrivals(copies):
    for copy, remote in copies:
        if remote:
            copy.wait_recv()
        else:
            copy.wait()


def wait_sends(hops, last):
    for hop in hops.values():
        hop.wait_send()
    for copies in last.values():
        for copy, remote in copies:
            if remote:
                copy.wait_send()


def exchange_in_kernel(produce, deliver, order, *scratch):
    hops, last = start_exchange(produce, deliver, order, lambda: None, *scratch)
    for copies in last.values():
        wait_arrivals(copies)
    wait_sends(hops, last)


def exchange_scratch(shape):
    return [
        pltpu.VMEM((2, 4, 8) + shape, jnp.bfloat16),
        pltpu.VMEM((2, 4, 8) + shape, jnp.bfloat16),
        pltpu.SemaphoreType.DMA((6,)),
        pltpu.SemaphoreType.DMA((6,)),
        pltpu.SemaphoreType.DMA((64,)),
        pltpu.SemaphoreType.DMA((64,)),
    ]


def slot_at(way, group, t):
    owner = group * 8 + t if way == 0 else (t // 2 * 4 + group) * 2 + lax.rem(t, 2)
    return owner * CAPACITY + way


def table_hops(table, send, recv):
    z, y, core = place()
    mine = y * 2 + core
    copies = []
    for d in (1, 3, 2):
        copies.append(
            pltpu.make_async_remote_copy(
                src_ref=table.at[mine, z],
                dst_ref=table.at[mine, z],
                send_sem=send.at[d - 1],
                recv_sem=recv.at[d - 1],
                device_id=device(lax.rem(z + d, 4), y, core),
                device_id_type=MESH,
            )
        )
        copies[-1].start()
    return copies


def table_spread(table, send, recv):
    z, y, core = place()
    mine = y * 2 + core
    copies = []
    for d in GROUP_ORDER:
        for dc in (0, 1):
            if d or dc:
                n = d * 2 + dc
                copies.append(
                    pltpu.make_async_remote_copy(
                        src_ref=table.at[mine],
                        dst_ref=table.at[mine],
                        send_sem=send.at[n],
                        recv_sem=recv.at[n],
                        device_id=device(z, lax.rem(y + d, 4), lax.rem(core + dc, 2)),
                        device_id_type=MESH,
                    )
                )
                copies[-1].start()
    return copies


def fetch_kernel(
    half_ref, request_ref, coef_hbm_ref, ints_hbm_ref,
    recv_ref, coef_ref, wanted_ref,
    own_coef_ref, own_coef_sem, ints_ref, ints_sem, table_ref, table_smem, table_sem,
    table_hop_send, table_hop_recv, table_last_send, table_last_recv,
    coef_send_ref, coef_transit_ref, coef_hop_send, coef_hop_recv, coef_last_send, coef_last_recv,
    plane_send, plane_recv,
    send_ref, transit_ref, *sems,
):
    z, y, core = place()
    here = (z, y)
    mine = lax.axis_index("aux")
    rows = coef_ref.shape[4]
    first = pl.multiple_of(mine * rows, rows)
    load_coef = pltpu.make_async_copy(coef_hbm_ref.at[:, pl.ds(first, rows)], own_coef_ref, own_coef_sem)
    load_coef.start()
    load = pltpu.make_async_copy(ints_hbm_ref, ints_ref, ints_sem)
    load.start()
    table_ref[y * 2 + core, z] = request_ref[...]
    greet()
    tables = table_hops(table_ref, table_hop_send, table_hop_recv)
    load_coef.wait()

    def pick(way, d, group):
        @pl.loop(0, 8)
        def _(t):
            coef_send_ref[way, group, t] = own_coef_ref[half_ref[slot_at(way, group, t)]]

    spread_tables = []

    def between():
        for copy in tables:
            copy.wait()
        spread_tables.extend(table_spread(table_ref, table_last_send, table_last_recv))

    coef_hops, coef_last = start_exchange(
        pick,
        lambda way, group, t: coef_ref.at[mine, way, group, t],
        OWN_FIRST,
        between,
        coef_send_ref, coef_transit_ref, coef_hop_send, coef_hop_recv, coef_last_send, coef_last_recv,
    )

    batches = [(way, (4 - d) % 4) for d in OWN_FIRST for way in (0, 1)]
    shared = {}

    def to_plane(way, ds, source, d, part, n):
        block = coef_ref.at[lax.rem(mine + source, 4), way, lax.rem(here[way] + 4 - ds, 4), part]
        n += (way * 4 + ds) * 4
        copy = pltpu.make_async_remote_copy(
            src_ref=block,
            dst_ref=block,
            send_sem=plane_send.at[n],
            recv_sem=plane_recv.at[n],
            device_id=plane(d),
            device_id_type=MESH,
        )
        copy.start()
        shared.setdefault((way, ds), []).append(copy)

    def share(way, ds):
        wait_arrivals(coef_last[way, ds])
        to_plane(way, ds, 0, 1, pl.ds(0, 8), 0)
        to_plane(way, ds, 0, 3, pl.ds(0, 8), 1)

    def pass_on(way, ds):
        shared[way, ds][0].wait_recv()
        to_plane(way, ds, 3, 1, pl.ds(0, 4), 2)
        shared[way, ds][1].wait_recv()
        to_plane(way, ds, 1, 3, pl.ds(4, 4), 3)

    share(*batches[0])
    share(*batches[1])
    pass_on(*batches[0])
    for copy in spread_tables:
        copy.wait()
    to_smem = pltpu.make_async_copy(table_ref, table_smem, table_sem)
    to_smem.start()
    to_smem.wait()
    load.wait()
    me = lax.axis_index("pair")

    def produce(way, d, group):
        n = batches.index((way, (4 - d) % 4))
        if n + 2 < len(batches):
            share(*batches[n + 2])
        if n + 1 < len(batches):
            pass_on(*batches[n + 1])
        for copy in shared[batches[n]][2:]:
            copy.wait_recv()

        @pl.loop(0, 8)
        def _(t):
            slot = slot_at(way, group, t)
            owner = slot // CAPACITY
            wanted = table_smem[lax.rem(owner, 8), owner // 8, 0, me * CAPACITY + way]
            wanted_ref[slot] = wanted
            coef = coef_ref[:, way, group, t].reshape(-1, coef_ref.shape[-1])
            send_ref[way, group, t] = lax.dot_general(
                coef, ints_ref[jnp.maximum(wanted - 1, 0)], (((0,), (0,)), ((), ())),
                preferred_element_type=jnp.float32,
            ).astype(send_ref.dtype)

    exchange_in_kernel(
        produce,
        lambda way, group, t: recv_ref.at[group * 8 + t if way == 0 else (t // 2 * 4 + group) * 2 + lax.rem(t, 2), way],
        OWN_FIRST,
        send_ref, transit_ref, *sems,
    )
    wait_sends(coef_hops, coef_last)
    for copies in shared.values():
        for copy in copies:
            copy.wait_send()


def couple_kernel(
    slot_ref, pair_ref, side_ref, partner_ref, occ_ref, count_ref, fock_ref, energy_in_ref, rows_ref,
    recv_ref, energy_ref,
    own_ref, part_ref, inbox_ref, weights_ref, sum_send, sum_recv, weight_send, weight_recv, energy_send, energy_recv,
    send_ref, transit_ref, *sems,
):
    share, width, _ = own_ref.shape
    pairs = count_ref.shape[0]
    mine = lax.axis_index("aux")
    greet()

    size = share // SUMMED_IN_PARTS

    def couplings(d, b, out_ref):
        first = lax.rem(mine + d, 4) * share + b * size

        @pl.loop(0, size)
        def _(t):
            k = jnp.minimum(first + t, pairs - 1)
            out_ref[b * size + t] = lax.dot_general(
                rows_ref[slot_ref[2 * k]],
                rows_ref[slot_ref[2 * k + 1]],
                (((1,), (1,)), ((), ())),
                preferred_element_type=jnp.float32,
            ).astype(out_ref.dtype)

    sums = {}
    for b in range(SUMMED_IN_PARTS):
        for d in (2, 1, 3):
            couplings(d, b, part_ref.at[d - 1])
            n = b * 3 + d - 1
            sums[b, d] = pltpu.make_async_remote_copy(
                src_ref=part_ref.at[d - 1, pl.ds(b * size, size)],
                dst_ref=inbox_ref.at[d - 1, pl.ds(b * size, size)],
                send_sem=sum_send.at[n],
                recv_sem=sum_recv.at[n],
                device_id=plane(d),
                device_id_type=MESH,
            )
            sums[b, d].start()
    for b in range(SUMMED_IN_PARTS):
        couplings(0, b, own_ref)

    row_id = lax.broadcasted_iota(jnp.int32, (width, width), 0)
    col_id = lax.broadcasted_iota(jnp.int32, (width, width), 1)

    def weigh(t):
        k = jnp.minimum(mine * share + t, pairs - 1)
        others = [inbox_ref[n, t].astype(jnp.float32) for n in range(3)]
        coupling = (own_ref[t] + others[0]) + (others[1] + others[2])
        by_col = jnp.broadcast_to(energy_in_ref[pl.ds(k, 1), :], (width, width))
        denom = by_col.T + by_col - fock_ref[occ_ref[2 * k]] - fock_ref[occ_ref[2 * k + 1]]
        inside = (row_id < count_ref[k]) & (col_id < count_ref[k])
        amplitude = jnp.where(inside, -coupling / denom, 0.0)
        mixed = 2.0 * amplitude - amplitude.T
        energy_ref[mine, pl.ds(t, 1), :] = jnp.sum(coupling * mixed, axis=0, keepdims=True)
        weights_ref[mine, t] = mixed.astype(jnp.bfloat16)

    copies = []

    def tell(ref, send, recv, n, d):
        copies.append(
            pltpu.make_async_remote_copy(
                src_ref=ref,
                dst_ref=ref,
                send_sem=send.at[n],
                recv_sem=recv.at[n],
                device_id=plane(d),
                device_id_type=MESH,
            )
        )
        copies[-1].start()

    for b in range(SUMMED_IN_PARTS):
        for d in (2, 1, 3):
            sums[b, d].wait_recv()
        pl.loop(b * size, (b + 1) * size)(weigh)
        for d in (2, 1, 3):
            tell(weights_ref.at[mine, pl.ds(b * size, size)], weight_send, weight_recv, b * 3 + d - 1, d)
    for d in (2, 1, 3):
        tell(energy_ref.at[mine], energy_send, energy_recv, d - 1, d)
    for copy in copies:
        copy.wait()
    for copy in sums.values():
        copy.wait_send()

    def produce(way, d, group):
        @pl.loop(0, 8)
        def _(t):
            slot = slot_at(way, group, t)
            pair = pair_ref[slot]
            weights = weights_ref[pair // share, lax.rem(pair, share)].astype(jnp.float32)
            weights = jnp.where(side_ref[slot] == 0, weights, weights.T).astype(jnp.bfloat16)
            send_ref[way, group, t] = jnp.dot(
                weights, rows_ref[partner_ref[slot]], preferred_element_type=jnp.float32
            ).astype(send_ref.dtype)

    exchange_in_kernel(
        produce, lambda way, group, t: recv_ref.at[way, group, t], OWN_FIRST, send_ref, transit_ref, *sems
    )


def grad_kernel(wanted_ref, coef_ref, gamma_ref, out_ref):
    step = pl.program_id(0)

    @pl.when(step == 0)
    def _():
        out_ref[...] = jnp.zeros_like(out_ref)

    for t in range(8):
        wanted = wanted_ref[slot_at_step(step, t)]
        coef = coef_ref[:, 0, 0, t].reshape(-1, coef_ref.shape[-1])
        coef = jnp.where(wanted > 0, coef, jnp.zeros_like(coef))
        term = jnp.dot(coef, gamma_ref[0, 0, t], preferred_element_type=jnp.float32).astype(jnp.bfloat16)
        out_ref[jnp.maximum(wanted - 1, 0)] += term.astype(jnp.float32)


def slot_at_step(step, t):
    group = lax.rem(step, 4)
    return jnp.where(step < 4, slot_at(0, group, t), slot_at(1, group, t))


def params(limit, collective_id=None):
    return pltpu.CompilerParams(
        vmem_limit_bytes=limit << 20, collective_id=collective_id, has_side_effects=collective_id is not None
    )


def local(three_index, fock_diag, pair_occ, pno_count, pno_energy, pno_coef):
    groups = lax.axis_size("pair")
    planes = lax.axis_size("aux")
    occ_dev, width_dom, width_aux = three_index.shape
    pair_dev = pair_occ.shape[0]
    width_pno = pno_coef.shape[3]
    halves = 2 * pair_dev
    slots = groups * CAPACITY
    part = width_dom // planes
    smem = pl.BlockSpec(memory_space=pltpu.SMEM)
    vmem = pl.BlockSpec(memory_space=pltpu.VMEM)
    hbm = pl.BlockSpec(memory_space=pl.ANY)

    slot_of, half_of, request, partner = plan_slots(pair_occ, groups, occ_dev)

    half = jnp.maximum(half_of, 0)
    coef_block = (part, width_pno)
    rows, coef, wanted = pl.pallas_call(
        fetch_kernel,
        name="fetch_coef_and_return_rows",
        out_shape=(
            pltpu.VMEM((groups, CAPACITY, width_pno, width_aux), jnp.bfloat16),
            jax.ShapeDtypeStruct((planes, CAPACITY, 4, 8, part, width_pno), jnp.bfloat16),
            jax.ShapeDtypeStruct((slots,), jnp.int32),
        ),
        in_specs=[smem, vmem, hbm, hbm],
        out_specs=(vmem, vmem, smem),
        scratch_shapes=[
            pltpu.VMEM((halves, part, width_pno), jnp.bfloat16),
            pltpu.SemaphoreType.DMA,
            pltpu.VMEM((occ_dev, width_dom, width_aux), jnp.bfloat16),
            pltpu.SemaphoreType.DMA,
            pltpu.VMEM((8, 4, 8, 128), jnp.int32),
            pltpu.SMEM((8, 4, 8, 128), jnp.int32),
            pltpu.SemaphoreType.DMA,
            pltpu.SemaphoreType.DMA((3,)),
            pltpu.SemaphoreType.DMA((3,)),
            pltpu.SemaphoreType.DMA((8,)),
            pltpu.SemaphoreType.DMA((8,)),
        ]
        + exchange_scratch(coef_block)
        + [pltpu.SemaphoreType.DMA((32,)), pltpu.SemaphoreType.DMA((32,))]
        + exchange_scratch((width_pno, width_aux)),
        compiler_params=params(49, 1),
    )(
        half,
        jnp.pad(request[None, :], ((0, 7), (0, 128 - slots))),
        pltpu.with_memory_space_constraint(pno_coef.reshape(halves, width_dom, width_pno), pltpu.HBM),
        pltpu.with_memory_space_constraint(three_index, pltpu.HBM),
    )
    rows = rows.reshape(slots, width_pno, width_aux)

    share = -(-pair_dev // planes)
    gamma, energy_cols = pl.pallas_call(
        couple_kernel,
        name="couple_and_return_gamma",
        out_shape=(
            jax.ShapeDtypeStruct((CAPACITY, 4, 8, width_pno, width_aux), jnp.bfloat16),
            jax.ShapeDtypeStruct((planes, share, width_pno), jnp.float32),
        ),
        in_specs=[smem] * 7 + [vmem] * 2,
        out_specs=(hbm, vmem),
        scratch_shapes=[
            pltpu.VMEM((share, width_pno, width_pno), jnp.float32),
            pltpu.VMEM((planes - 1, share, width_pno, width_pno), jnp.bfloat16),
            pltpu.VMEM((planes - 1, share, width_pno, width_pno), jnp.bfloat16),
            pltpu.VMEM((planes, share, width_pno, width_pno), jnp.bfloat16),
        ]
        + [pltpu.SemaphoreType.DMA((SUMMED_IN_PARTS * (planes - 1),))] * 4
        + [pltpu.SemaphoreType.DMA((planes - 1,))] * 2
        + exchange_scratch((width_pno, width_aux)),
        compiler_params=params(49, 2),
    )(slot_of, half // 2, half % 2, partner, pair_occ.reshape(halves), pno_count, fock_diag, pno_energy, rows)
    energy = jnp.sum(energy_cols, axis=2).reshape(-1)[:pair_dev] / (width_pno * width_pno)
    grad = pl.pallas_call(
        grad_kernel,
        name="add_terms",
        out_shape=jax.ShapeDtypeStruct((occ_dev, width_dom, width_aux), jnp.float32),
        grid_spec=pltpu.PrefetchScalarGridSpec(
            num_scalar_prefetch=1,
            grid=(8,),
            in_specs=[
                pl.BlockSpec((planes, 1, 1, 8, part, width_pno), lambda s, w: (0, s // 4, s % 4, 0, 0, 0)),
                pl.BlockSpec((1, 1, 8, width_pno, width_aux), lambda s, w: (s // 4, s % 4, 0, 0, 0)),
            ],
            out_specs=pl.BlockSpec((occ_dev, width_dom, width_aux), lambda s, w: (0, 0, 0)),
        ),
        compiler_params=params(49),
    )(wanted, *(pltpu.with_memory_space_constraint(x, pltpu.HBM) for x in (coef, gamma)))
    return energy, grad


def solution(mesh):
    placed = (
        P("pair", None, "aux"),
        P(),
        P("pair", None),
        P("pair"),
        P("pair", None),
        P("pair", None, None, None),
    )
    return jax.shard_map(
        local,
        mesh=mesh,
        in_specs=placed,
        out_specs=(P("pair"), P("pair", None, "aux")),
        check_vma=False,
    )
```

```python
import functools

import jax
import jax.numpy as jnp
from jax import lax
from jax.experimental import pallas as pl
from jax.experimental.pallas import tpu as pltpu
from jax.sharding import PartitionSpec as P

CAPACITY = 2
MESH = pl.DeviceIdType.MESH
GROUP_ORDER = (1, 3, 2, 0)
OWN_FIRST = (0, 1, 3, 2)
SUMMED_IN_PARTS = 2


def plan_slots(pair_occ, groups, occ_dev):
    occ_flat = pair_occ.reshape(-1)
    halves = occ_flat.shape[0]
    owner = occ_flat // occ_dev
    half_ids = jnp.arange(halves, dtype=jnp.int32)
    earlier = (owner[None, :] == owner[:, None]) & (half_ids[None, :] < half_ids[:, None])
    rank = jnp.sum(earlier.astype(jnp.int32), axis=1)
    slot_of = owner * CAPACITY + rank
    hot = (slot_of[None, :] == jnp.arange(groups * CAPACITY, dtype=jnp.int32)[:, None]).astype(jnp.int32)
    half_of = jnp.sum(hot * (half_ids + 1)[None, :], axis=1) - 1
    request = jnp.sum(hot * (occ_flat % occ_dev + 1)[None, :], axis=1)
    partner = jnp.sum(hot * slot_of.reshape(-1, 2)[:, ::-1].reshape(-1)[None, :], axis=1)
    return slot_of, half_of, request, partner


def place():
    me = lax.axis_index("pair")
    return me // 8, lax.rem(me // 2, 4), lax.rem(me, 2)


def device(z, y, core):
    return {"pair": (z * 4 + y) * 2 + core}


def plane(d):
    return {"aux": lax.rem(lax.axis_index("aux") + d, 4)}


def greet():
    z, y, core = place()
    barrier = pltpu.get_barrier_semaphore()
    peers = [device(z, y, 1 - core)]
    for d in (1, 2, 3):
        peers.append(plane(d))
        for c in (core, 1 - core):
            peers += [device(lax.rem(z + d, 4), y, c), device(z, lax.rem(y + d, 4), c)]
    for peer in peers:
        pl.semaphore_signal(barrier, inc=1, device_id=peer, device_id_type=MESH)
    pl.semaphore_wait(barrier, len(peers))


def start_exchange(produce, deliver, order, between, last, send, transit, hop_send, hop_recv, last_send, last_recv):
    z, y, core = place()
    here, across = (z, y), (y, z)
    hops = {}

    def hop(way, d):
        group, n = lax.rem(here[way] + d, 4), way * 3 + d - 1
        hops[way, d] = pltpu.make_async_remote_copy(
            src_ref=send.at[way, group],
            dst_ref=transit.at[way, here[way]],
            send_sem=hop_send.at[n],
            recv_sem=hop_recv.at[n],
            device_id=device(group, y, core) if way == 0 else device(z, group, core),
            device_id_type=MESH,
        )
        hops[way, d].start()

    def spread(way, ds):
        source = lax.rem(here[way] + 4 - ds, 4)
        last[way, ds] = []
        for d in GROUP_ORDER:
            for dc in (0, 1):
                to, to_core = lax.rem(across[way] + d, 4), lax.rem(core + dc, 2)
                block = (transit if ds else send).at[way, source, to * 2 + to_core]
                dst = deliver(way, source, across[way] * 2 + core)
                n = ((way * 4 + ds) * 4 + d) * 2 + dc
                if d == 0 and dc == 0:
                    copy = pltpu.make_async_copy(block, dst, last_send.at[n])
                else:
                    copy = pltpu.make_async_remote_copy(
                        src_ref=block,
                        dst_ref=dst,
                        send_sem=last_send.at[n],
                        recv_sem=last_recv.at[n],
                        device_id=device(z, to, to_core) if way == 0 else device(to, y, to_core),
                        device_id_type=MESH,
                    )
                copy.start()
                last[way, ds].append((copy, d > 0 or dc > 0))

    for d in order:
        for way in (0, 1):
            produce(way, d, lax.rem(here[way] + d, 4))
            if d:
                hop(way, d)
            else:
                spread(way, 0)
    between()
    for ds in (1, 3, 2):
        for way in (0, 1):
            hops[way, ds].wait_recv()
            spread(way, ds)
    return hops, last


def wait_arrivals(copies):
    for copy, remote in copies:
        if remote:
            copy.wait_recv()
        else:
            copy.wait()


def wait_sends(hops, last):
    for hop in hops.values():
        hop.wait_send()
    for copies in last.values():
        for copy, remote in copies:
            if remote:
                copy.wait_send()


def exchange_in_kernel(produce, deliver, order, *scratch):
    hops, last = start_exchange(produce, deliver, order, lambda: None, {}, *scratch)
    for copies in last.values():
        wait_arrivals(copies)
    wait_sends(hops, last)


def exchange_scratch(shape):
    return [
        pltpu.VMEM((2, 4, 8) + shape, jnp.bfloat16),
        pltpu.VMEM((2, 4, 8) + shape, jnp.bfloat16),
        pltpu.SemaphoreType.DMA((6,)),
        pltpu.SemaphoreType.DMA((6,)),
        pltpu.SemaphoreType.DMA((64,)),
        pltpu.SemaphoreType.DMA((64,)),
    ]


def slot_at(way, group, t):
    owner = group * 8 + t if way == 0 else (t // 2 * 4 + group) * 2 + lax.rem(t, 2)
    return owner * CAPACITY + way


def table_hops(table, send, recv):
    z, y, core = place()
    mine = y * 2 + core
    copies = []
    for d in (1, 3, 2):
        copies.append(
            pltpu.make_async_remote_copy(
                src_ref=table.at[mine, z],
                dst_ref=table.at[mine, z],
                send_sem=send.at[d - 1],
                recv_sem=recv.at[d - 1],
                device_id=device(lax.rem(z + d, 4), y, core),
                device_id_type=MESH,
            )
        )
        copies[-1].start()
    return copies


def table_spread(table, send, recv):
    z, y, core = place()
    mine = y * 2 + core
    copies = []
    for d in GROUP_ORDER:
        for dc in (0, 1):
            if d or dc:
                n = d * 2 + dc
                copies.append(
                    pltpu.make_async_remote_copy(
                        src_ref=table.at[mine],
                        dst_ref=table.at[mine],
                        send_sem=send.at[n],
                        recv_sem=recv.at[n],
                        device_id=device(z, lax.rem(y + d, 4), lax.rem(core + dc, 2)),
                        device_id_type=MESH,
                    )
                )
                copies[-1].start()
    return copies


def fetch_rows(
    half_ref, request_ref, coef_hbm_ref, ints_hbm_ref,
    rows_ref, coef_ref, wanted_ref,
    own_coef_ref, own_coef_sem, ints_ref, ints_sem, table_ref, table_smem, table_sem,
    table_hop_send, table_hop_recv, table_last_send, table_last_recv,
    coef_send_ref, coef_transit_ref, coef_hop_send, coef_hop_recv, coef_last_send, coef_last_recv,
    plane_send, plane_recv,
    *exchange,
):
    send_ref = exchange[0]
    z, y, core = place()
    here = (z, y)
    mine = lax.axis_index("aux")
    rows = coef_ref.shape[4]
    first = pl.multiple_of(mine * rows, rows)
    load_coef = pltpu.make_async_copy(coef_hbm_ref.at[:, pl.ds(first, rows)], own_coef_ref, own_coef_sem)
    load_coef.start()
    load = pltpu.make_async_copy(ints_hbm_ref, ints_ref, ints_sem)
    load.start()
    table_ref[y * 2 + core, z] = request_ref[...]
    greet()
    tables = table_hops(table_ref, table_hop_send, table_hop_recv)
    load_coef.wait()

    def pick(way, d, group):
        @pl.loop(0, 8)
        def _(t):
            coef_send_ref[way, group, t] = own_coef_ref[half_ref[slot_at(way, group, t)]]

    spread_tables = []
    coef_last = {}
    batches = [(way, (4 - d) % 4) for d in OWN_FIRST for way in (0, 1)]
    shared = {}

    def to_plane(way, ds, source, d, part, n):
        block = coef_ref.at[lax.rem(mine + source, 4), way, lax.rem(here[way] + 4 - ds, 4), part]
        n += (way * 4 + ds) * 4
        copy = pltpu.make_async_remote_copy(
            src_ref=block,
            dst_ref=block,
            send_sem=plane_send.at[n],
            recv_sem=plane_recv.at[n],
            device_id=plane(d),
            device_id_type=MESH,
        )
        copy.start()
        shared.setdefault((way, ds), []).append(copy)

    def share(way, ds):
        wait_arrivals(coef_last[way, ds])
        to_plane(way, ds, 0, 1, pl.ds(0, 8), 0)
        to_plane(way, ds, 0, 3, pl.ds(0, 8), 1)

    def pass_on(way, ds):
        shared[way, ds][0].wait_recv()
        to_plane(way, ds, 3, 1, pl.ds(0, 4), 2)
        shared[way, ds][1].wait_recv()
        to_plane(way, ds, 1, 3, pl.ds(4, 4), 3)

    def between():
        for copy in tables:
            copy.wait()
        spread_tables.extend(table_spread(table_ref, table_last_send, table_last_recv))
        share(*batches[0])
        share(*batches[1])

    coef_hops, _ = start_exchange(
        pick,
        lambda way, group, t: coef_ref.at[mine, way, group, t],
        OWN_FIRST,
        between,
        coef_last,
        coef_send_ref, coef_transit_ref, coef_hop_send, coef_hop_recv, coef_last_send, coef_last_recv,
    )

    pass_on(*batches[0])
    for copy in spread_tables:
        copy.wait()
    to_smem = pltpu.make_async_copy(table_ref, table_smem, table_sem)
    to_smem.start()
    to_smem.wait()
    load.wait()
    me = lax.axis_index("pair")

    def produce(way, d, group):
        n = batches.index((way, (4 - d) % 4))
        if n + 2 < len(batches):
            share(*batches[n + 2])
        if n + 1 < len(batches):
            pass_on(*batches[n + 1])
        for copy in shared[batches[n]][2:]:
            copy.wait_recv()

        @pl.loop(0, 8)
        def _(t):
            slot = slot_at(way, group, t)
            owner = slot // CAPACITY
            wanted = table_smem[lax.rem(owner, 8), owner // 8, 0, me * CAPACITY + way]
            wanted_ref[slot] = wanted
            coef = coef_ref[:, way, group, t].reshape(-1, coef_ref.shape[-1])
            send_ref[way, group, t] = lax.dot_general(
                coef, ints_ref[jnp.maximum(wanted - 1, 0)], (((0,), (0,)), ((), ())),
                preferred_element_type=jnp.float32,
            ).astype(send_ref.dtype)

    exchange_in_kernel(
        produce,
        lambda way, group, t: rows_ref.at[slot_at(way, group, t)],
        OWN_FIRST,
        *exchange,
    )
    wait_sends(coef_hops, coef_last)
    for copies in shared.values():
        for copy in copies:
            copy.wait_send()


def couple_and_weigh(
    slot_ref, pair_ref, side_ref, partner_ref, occ_ref, count_ref, fock_ref, energy_in_ref, rows_ref,
    recv_ref, energy_ref,
    own_ref, part_ref, inbox_ref, weights_ref, sum_send, sum_recv, weight_send, weight_recv, energy_send, energy_recv,
    *exchange,
):
    share, width, _ = own_ref.shape
    pairs = count_ref.shape[0]
    mine = lax.axis_index("aux")
    send_ref = exchange[0]

    size = share // SUMMED_IN_PARTS

    def couplings(d, b, out_ref):
        first = lax.rem(mine + d, 4) * share + b * size

        @pl.loop(0, size)
        def _(t):
            k = jnp.minimum(first + t, pairs - 1)
            out_ref[b * size + t] = lax.dot_general(
                rows_ref[slot_ref[2 * k]],
                rows_ref[slot_ref[2 * k + 1]],
                (((1,), (1,)), ((), ())),
                preferred_element_type=jnp.float32,
            ).astype(out_ref.dtype)

    sums = {}
    for b in range(SUMMED_IN_PARTS):
        for d in (2, 1, 3):
            couplings(d, b, part_ref.at[d - 1])
            n = b * 3 + d - 1
            sums[b, d] = pltpu.make_async_remote_copy(
                src_ref=part_ref.at[d - 1, pl.ds(b * size, size)],
                dst_ref=inbox_ref.at[d - 1, pl.ds(b * size, size)],
                send_sem=sum_send.at[n],
                recv_sem=sum_recv.at[n],
                device_id=plane(d),
                device_id_type=MESH,
            )
            sums[b, d].start()
    for b in range(SUMMED_IN_PARTS):
        couplings(0, b, own_ref)

    row_id = lax.broadcasted_iota(jnp.int32, (width, width), 0)
    col_id = lax.broadcasted_iota(jnp.int32, (width, width), 1)

    def weigh(t):
        k = jnp.minimum(mine * share + t, pairs - 1)
        others = [inbox_ref[n, t].astype(jnp.float32) for n in range(3)]
        coupling = (own_ref[t] + others[0]) + (others[1] + others[2])
        by_col = jnp.broadcast_to(energy_in_ref[pl.ds(k, 1), :], (width, width))
        denom = by_col.T + by_col - fock_ref[occ_ref[2 * k]] - fock_ref[occ_ref[2 * k + 1]]
        inside = (row_id < count_ref[k]) & (col_id < count_ref[k])
        amplitude = jnp.where(inside, -coupling / denom, 0.0)
        mixed = 2.0 * amplitude - amplitude.T
        energy_ref[mine, pl.ds(t, 1), :] = jnp.sum(coupling * mixed, axis=0, keepdims=True)
        weights_ref[mine, t] = mixed.astype(jnp.bfloat16)

    copies = []

    def tell(ref, send, recv, n, d):
        copies.append(
            pltpu.make_async_remote_copy(
                src_ref=ref,
                dst_ref=ref,
                send_sem=send.at[n],
                recv_sem=recv.at[n],
                device_id=plane(d),
                device_id_type=MESH,
            )
        )
        copies[-1].start()

    for b in range(SUMMED_IN_PARTS):
        for d in (2, 1, 3):
            sums[b, d].wait_recv()
        pl.loop(b * size, (b + 1) * size)(weigh)
        for d in (2, 1, 3):
            tell(weights_ref.at[mine, pl.ds(b * size, size)], weight_send, weight_recv, b * 3 + d - 1, d)
    for d in (2, 1, 3):
        tell(energy_ref.at[mine], energy_send, energy_recv, d - 1, d)
    for copy in copies:
        copy.wait()
    for copy in sums.values():
        copy.wait_send()

    def produce(way, d, group):
        @pl.loop(0, 8)
        def _(t):
            slot = slot_at(way, group, t)
            pair = pair_ref[slot]
            weights = weights_ref[pair // share, lax.rem(pair, share)].astype(jnp.float32)
            weights = jnp.where(side_ref[slot] == 0, weights, weights.T).astype(jnp.bfloat16)
            send_ref[way, group, t] = jnp.dot(
                weights, rows_ref[partner_ref[slot]], preferred_element_type=jnp.float32
            ).astype(send_ref.dtype)

    exchange_in_kernel(
        produce, lambda way, group, t: recv_ref.at[way, group, t], OWN_FIRST, *exchange
    )


def pairs_kernel(
    half_ref, slot_ref, pair_ref, side_ref, partner_ref, occ_ref, count_ref, fock_ref, request_ref, energy_in_ref,
    coef_hbm_ref, ints_hbm_ref,
    gamma_ref, coef_ref, wanted_ref, energy_ref,
    rows_ref, *scratch,
):
    fetch, couple, (send_ref, transit_rows, transit_gamma), sems = scratch[:19], scratch[19:29], scratch[29:32], scratch[32:]
    fetch_rows(
        half_ref, request_ref, coef_hbm_ref, ints_hbm_ref, rows_ref, coef_ref, wanted_ref, *fetch,
        send_ref, transit_rows, *sems[:4],
    )
    couple_and_weigh(
        slot_ref, pair_ref, side_ref, partner_ref, occ_ref, count_ref, fock_ref, energy_in_ref, rows_ref,
        gamma_ref, energy_ref, *couple,
        send_ref, transit_gamma, *sems[4:],
    )


def grad_kernel(wanted_ref, coef_ref, gamma_ref, out_ref):
    step = pl.program_id(0)

    @pl.when(step == 0)
    def _():
        out_ref[...] = jnp.zeros_like(out_ref)

    for t in range(8):
        wanted = wanted_ref[slot_at_step(step, t)]
        coef = coef_ref[:, 0, 0, t].reshape(-1, coef_ref.shape[-1])
        coef = jnp.where(wanted > 0, coef, jnp.zeros_like(coef))
        term = jnp.dot(coef, gamma_ref[0, 0, t], preferred_element_type=jnp.float32).astype(jnp.bfloat16)
        out_ref[jnp.maximum(wanted - 1, 0)] += term.astype(jnp.float32)


def slot_at_step(step, t):
    group = lax.rem(step, 4)
    return jnp.where(step < 4, slot_at(0, group, t), slot_at(1, group, t))


def params(limit, collective_id=None):
    return pltpu.CompilerParams(
        vmem_limit_bytes=limit << 20, collective_id=collective_id, has_side_effects=collective_id is not None
    )


def local(three_index, fock_diag, pair_occ, pno_count, pno_energy, pno_coef):
    groups = lax.axis_size("pair")
    planes = lax.axis_size("aux")
    occ_dev, width_dom, width_aux = three_index.shape
    pair_dev = pair_occ.shape[0]
    width_pno = pno_coef.shape[3]
    halves = 2 * pair_dev
    slots = groups * CAPACITY
    part = width_dom // planes
    smem = pl.BlockSpec(memory_space=pltpu.SMEM)
    vmem = pl.BlockSpec(memory_space=pltpu.VMEM)
    hbm = pl.BlockSpec(memory_space=pl.ANY)

    slot_of, half_of, request, partner = plan_slots(pair_occ, groups, occ_dev)

    half = jnp.maximum(half_of, 0)
    coef_block = (part, width_pno)
    share = -(-pair_dev // planes)
    row_block = exchange_scratch((width_pno, width_aux))
    gamma, coef, wanted, energy_cols = pl.pallas_call(
        pairs_kernel,
        name="pairs",
        out_shape=(
            jax.ShapeDtypeStruct((CAPACITY, 4, 8, width_pno, width_aux), jnp.bfloat16),
            jax.ShapeDtypeStruct((planes, CAPACITY, 4, 8, part, width_pno), jnp.bfloat16),
            jax.ShapeDtypeStruct((slots,), jnp.int32),
            jax.ShapeDtypeStruct((planes, share, width_pno), jnp.float32),
        ),
        in_specs=[smem] * 8 + [vmem] * 2 + [hbm] * 2,
        out_specs=(hbm, vmem, smem, vmem),
        scratch_shapes=[
            pltpu.VMEM((slots, width_pno, width_aux), jnp.bfloat16),
            pltpu.VMEM((halves, part, width_pno), jnp.bfloat16),
            pltpu.SemaphoreType.DMA,
            pltpu.VMEM((occ_dev, width_dom, width_aux), jnp.bfloat16),
            pltpu.SemaphoreType.DMA,
            pltpu.VMEM((8, 4, 8, 128), jnp.int32),
            pltpu.SMEM((8, 4, 8, 128), jnp.int32),
            pltpu.SemaphoreType.DMA,
            pltpu.SemaphoreType.DMA((3,)),
            pltpu.SemaphoreType.DMA((3,)),
            pltpu.SemaphoreType.DMA((8,)),
            pltpu.SemaphoreType.DMA((8,)),
        ]
        + exchange_scratch(coef_block)
        + [pltpu.SemaphoreType.DMA((32,)), pltpu.SemaphoreType.DMA((32,))]
        + [
            pltpu.VMEM((share, width_pno, width_pno), jnp.float32),
            pltpu.VMEM((planes - 1, share, width_pno, width_pno), jnp.bfloat16),
            pltpu.VMEM((planes - 1, share, width_pno, width_pno), jnp.bfloat16),
            pltpu.VMEM((planes, share, width_pno, width_pno), jnp.bfloat16),
        ]
        + [pltpu.SemaphoreType.DMA((SUMMED_IN_PARTS * (planes - 1),))] * 4
        + [pltpu.SemaphoreType.DMA((planes - 1,))] * 2
        + row_block[:1]
        + row_block[1:2] * 2
        + row_block[2:] * 2,
        compiler_params=params(56, 1),
    )(
        half, slot_of, half // 2, half % 2, partner, pair_occ.reshape(halves), pno_count, fock_diag,
        jnp.pad(request[None, :], ((0, 7), (0, 128 - slots))), pno_energy,
        pltpu.with_memory_space_constraint(pno_coef.reshape(halves, width_dom, width_pno), pltpu.HBM),
        pltpu.with_memory_space_constraint(three_index, pltpu.HBM),
    )
    energy = jnp.sum(energy_cols, axis=2).reshape(-1)[:pair_dev] / (width_pno * width_pno)
    grad = pl.pallas_call(
        grad_kernel,
        name="add_terms",
        out_shape=jax.ShapeDtypeStruct((occ_dev, width_dom, width_aux), jnp.float32),
        grid_spec=pltpu.PrefetchScalarGridSpec(
            num_scalar_prefetch=1,
            grid=(8,),
            in_specs=[
                pl.BlockSpec((planes, 1, 1, 8, part, width_pno), lambda s, w: (0, s // 4, s % 4, 0, 0, 0)),
                pl.BlockSpec((1, 1, 8, width_pno, width_aux), lambda s, w: (s // 4, s % 4, 0, 0, 0)),
            ],
            out_specs=pl.BlockSpec((occ_dev, width_dom, width_aux), lambda s, w: (0, 0, 0)),
        ),
        compiler_params=params(49),
    )(wanted, *(pltpu.with_memory_space_constraint(x, pltpu.HBM) for x in (coef, gamma)))
    return energy, grad


def solution(mesh):
    placed = (
        P("pair", None, "aux"),
        P(),
        P("pair", None),
        P("pair"),
        P("pair", None),
        P("pair", None, None, None),
    )
    return jax.shard_map(
        local,
        mesh=mesh,
        in_specs=placed,
        out_specs=(P("pair"), P("pair", None, "aux")),
        check_vma=False,
    )
```

```python
import functools

import jax
import jax.numpy as jnp
from jax import lax
from jax.experimental import pallas as pl
from jax.experimental.pallas import tpu as pltpu
from jax.sharding import PartitionSpec as P

CAPACITY = 2
MESH = pl.DeviceIdType.MESH
GROUP_ORDER = (1, 3, 2, 0)
OWN_FIRST = (0, 1, 3, 2)
SUMMED_IN_PARTS = 4


def plan_slots(pair_occ, groups, occ_dev):
    occ_flat = pair_occ.reshape(-1)
    halves = occ_flat.shape[0]
    owner = occ_flat // occ_dev
    half_ids = jnp.arange(halves, dtype=jnp.int32)
    earlier = (owner[None, :] == owner[:, None]) & (half_ids[None, :] < half_ids[:, None])
    rank = jnp.sum(earlier.astype(jnp.int32), axis=1)
    slot_of = owner * CAPACITY + rank
    hot = (slot_of[None, :] == jnp.arange(groups * CAPACITY, dtype=jnp.int32)[:, None]).astype(jnp.int32)
    half_of = jnp.sum(hot * (half_ids + 1)[None, :], axis=1) - 1
    request = jnp.sum(hot * (occ_flat % occ_dev + 1)[None, :], axis=1)
    partner = jnp.sum(hot * slot_of.reshape(-1, 2)[:, ::-1].reshape(-1)[None, :], axis=1)
    return slot_of, half_of, request, partner


def place():
    me = lax.axis_index("pair")
    return me // 8, lax.rem(me // 2, 4), lax.rem(me, 2)


def device(z, y, core):
    return {"pair": (z * 4 + y) * 2 + core}


def plane(d):
    return {"aux": lax.rem(lax.axis_index("aux") + d, 4)}


def greet():
    z, y, core = place()
    barrier = pltpu.get_barrier_semaphore()
    peers = [device(z, y, 1 - core)]
    for d in (1, 2, 3):
        peers.append(plane(d))
        for c in (core, 1 - core):
            peers += [device(lax.rem(z + d, 4), y, c), device(z, lax.rem(y + d, 4), c)]
    for peer in peers:
        pl.semaphore_signal(barrier, inc=1, device_id=peer, device_id_type=MESH)
    pl.semaphore_wait(barrier, len(peers))


def start_exchange(produce, deliver, order, between, last, send, transit, hop_send, hop_recv, last_send, last_recv):
    z, y, core = place()
    here, across = (z, y), (y, z)
    hops = {}

    def hop(way, d):
        group, n = lax.rem(here[way] + d, 4), way * 3 + d - 1
        hops[way, d] = pltpu.make_async_remote_copy(
            src_ref=send.at[way, group],
            dst_ref=transit.at[way, here[way]],
            send_sem=hop_send.at[n],
            recv_sem=hop_recv.at[n],
            device_id=device(group, y, core) if way == 0 else device(z, group, core),
            device_id_type=MESH,
        )
        hops[way, d].start()

    def spread(way, ds):
        source = lax.rem(here[way] + 4 - ds, 4)
        last[way, ds] = []
        for d in GROUP_ORDER:
            for dc in (0, 1):
                to, to_core = lax.rem(across[way] + d, 4), lax.rem(core + dc, 2)
                block = (transit if ds else send).at[way, source, to * 2 + to_core]
                dst = deliver(way, source, across[way] * 2 + core)
                n = ((way * 4 + ds) * 4 + d) * 2 + dc
                if d == 0 and dc == 0:
                    copy = pltpu.make_async_copy(block, dst, last_send.at[n])
                else:
                    copy = pltpu.make_async_remote_copy(
                        src_ref=block,
                        dst_ref=dst,
                        send_sem=last_send.at[n],
                        recv_sem=last_recv.at[n],
                        device_id=device(z, to, to_core) if way == 0 else device(to, y, to_core),
                        device_id_type=MESH,
                    )
                copy.start()
                last[way, ds].append((copy, d > 0 or dc > 0))

    for d in order:
        for way in (0, 1):
            produce(way, d, lax.rem(here[way] + d, 4))
            if d:
                hop(way, d)
            else:
                spread(way, 0)
    between()
    for ds in (1, 3, 2):
        for way in (0, 1):
            hops[way, ds].wait_recv()
            spread(way, ds)
    return hops, last


def wait_arrivals(copies):
    for copy, remote in copies:
        if remote:
            copy.wait_recv()
        else:
            copy.wait()


def wait_sends(hops, last):
    for hop in hops.values():
        hop.wait_send()
    for copies in last.values():
        for copy, remote in copies:
            if remote:
                copy.wait_send()


def exchange_in_kernel(produce, deliver, order, *scratch):
    hops, last = start_exchange(produce, deliver, order, lambda: None, {}, *scratch)
    for copies in last.values():
        wait_arrivals(copies)
    wait_sends(hops, last)


def exchange_scratch(shape):
    return [
        pltpu.VMEM((2, 4, 8) + shape, jnp.bfloat16),
        pltpu.VMEM((2, 4, 8) + shape, jnp.bfloat16),
        pltpu.SemaphoreType.DMA((6,)),
        pltpu.SemaphoreType.DMA((6,)),
        pltpu.SemaphoreType.DMA((64,)),
        pltpu.SemaphoreType.DMA((64,)),
    ]


def slot_at(way, group, t):
    owner = group * 8 + t if way == 0 else (t // 2 * 4 + group) * 2 + lax.rem(t, 2)
    return owner * CAPACITY + way


def table_hops(table, send, recv):
    z, y, core = place()
    mine = y * 2 + core
    copies = []
    for d in (1, 3, 2):
        copies.append(
            pltpu.make_async_remote_copy(
                src_ref=table.at[mine, z],
                dst_ref=table.at[mine, z],
                send_sem=send.at[d - 1],
                recv_sem=recv.at[d - 1],
                device_id=device(lax.rem(z + d, 4), y, core),
                device_id_type=MESH,
            )
        )
        copies[-1].start()
    return copies


def table_spread(table, send, recv):
    z, y, core = place()
    mine = y * 2 + core
    copies = []
    for d in GROUP_ORDER:
        for dc in (0, 1):
            if d or dc:
                n = d * 2 + dc
                copies.append(
                    pltpu.make_async_remote_copy(
                        src_ref=table.at[mine],
                        dst_ref=table.at[mine],
                        send_sem=send.at[n],
                        recv_sem=recv.at[n],
                        device_id=device(z, lax.rem(y + d, 4), lax.rem(core + dc, 2)),
                        device_id_type=MESH,
                    )
                )
                copies[-1].start()
    return copies


def fetch_rows(
    half_ref, request_ref, coef_hbm_ref, ints_hbm_ref,
    rows_ref, coef_ref, wanted_ref,
    own_coef_ref, own_coef_sem, ints_ref, ints_sem, table_ref, table_smem, table_sem,
    table_hop_send, table_hop_recv, table_last_send, table_last_recv,
    coef_send_ref, coef_transit_ref, coef_hop_send, coef_hop_recv, coef_last_send, coef_last_recv,
    plane_send, plane_recv,
    *exchange,
):
    send_ref = exchange[0]
    z, y, core = place()
    here = (z, y)
    mine = lax.axis_index("aux")
    rows = coef_ref.shape[4]
    first = pl.multiple_of(mine * rows, rows)
    load_coef = pltpu.make_async_copy(coef_hbm_ref.at[:, pl.ds(first, rows)], own_coef_ref, own_coef_sem)
    load_coef.start()
    load = pltpu.make_async_copy(ints_hbm_ref, ints_ref, ints_sem)
    load.start()
    table_ref[y * 2 + core, z] = request_ref[...]
    greet()
    tables = table_hops(table_ref, table_hop_send, table_hop_recv)
    load_coef.wait()

    def pick(way, d, group):
        @pl.loop(0, 8)
        def _(t):
            coef_send_ref[way, group, t] = own_coef_ref[half_ref[slot_at(way, group, t)]]

    spread_tables = []
    coef_last = {}
    batches = [(way, (4 - d) % 4) for d in OWN_FIRST for way in (0, 1)]
    shared = {}

    def to_plane(way, ds, source, d, part, n):
        block = coef_ref.at[lax.rem(mine + source, 4), way, lax.rem(here[way] + 4 - ds, 4), part]
        n += (way * 4 + ds) * 4
        copy = pltpu.make_async_remote_copy(
            src_ref=block,
            dst_ref=block,
            send_sem=plane_send.at[n],
            recv_sem=plane_recv.at[n],
            device_id=plane(d),
            device_id_type=MESH,
        )
        copy.start()
        shared.setdefault((way, ds), []).append(copy)

    def share(way, ds):
        wait_arrivals(coef_last[way, ds])
        to_plane(way, ds, 0, 1, pl.ds(0, 8), 0)
        to_plane(way, ds, 0, 3, pl.ds(0, 8), 1)

    def pass_on(way, ds):
        shared[way, ds][0].wait_recv()
        to_plane(way, ds, 3, 1, pl.ds(0, 4), 2)
        shared[way, ds][1].wait_recv()
        to_plane(way, ds, 1, 3, pl.ds(4, 4), 3)

    def between():
        for copy in tables:
            copy.wait()
        spread_tables.extend(table_spread(table_ref, table_last_send, table_last_recv))
        share(*batches[0])
        share(*batches[1])

    coef_hops, _ = start_exchange(
        pick,
        lambda way, group, t: coef_ref.at[mine, way, group, t],
        OWN_FIRST,
        between,
        coef_last,
        coef_send_ref, coef_transit_ref, coef_hop_send, coef_hop_recv, coef_last_send, coef_last_recv,
    )

    pass_on(*batches[0])
    for copy in spread_tables:
        copy.wait()
    to_smem = pltpu.make_async_copy(table_ref, table_smem, table_sem)
    to_smem.start()
    to_smem.wait()
    load.wait()
    me = lax.axis_index("pair")

    def produce(way, d, group):
        n = batches.index((way, (4 - d) % 4))
        if n + 2 < len(batches):
            share(*batches[n + 2])
        if n + 1 < len(batches):
            pass_on(*batches[n + 1])
        for copy in shared[batches[n]][2:]:
            copy.wait_recv()

        @pl.loop(0, 8)
        def _(t):
            slot = slot_at(way, group, t)
            owner = slot // CAPACITY
            wanted = table_smem[lax.rem(owner, 8), owner // 8, 0, me * CAPACITY + way]
            wanted_ref[slot] = wanted
            coef = coef_ref[:, way, group, t].reshape(-1, coef_ref.shape[-1])
            send_ref[way, group, t] = lax.dot_general(
                coef, ints_ref[jnp.maximum(wanted - 1, 0)], (((0,), (0,)), ((), ())),
                preferred_element_type=jnp.float32,
            ).astype(send_ref.dtype)

    exchange_in_kernel(
        produce,
        lambda way, group, t: rows_ref.at[slot_at(way, group, t)],
        OWN_FIRST,
        *exchange,
    )
    wait_sends(coef_hops, coef_last)
    for copies in shared.values():
        for copy in copies:
            copy.wait_send()


def couple_and_weigh(
    slot_ref, pair_ref, side_ref, partner_ref, occ_ref, count_ref, fock_ref, energy_in_ref, rows_ref,
    recv_ref, energy_ref,
    own_ref, part_ref, inbox_ref, weights_ref, sum_send, sum_recv, weight_send, weight_recv, energy_send, energy_recv,
    *exchange,
):
    share, width, _ = own_ref.shape
    pairs = count_ref.shape[0]
    mine = lax.axis_index("aux")
    send_ref = exchange[0]

    size = share // SUMMED_IN_PARTS

    def couplings(d, b, out_ref):
        first = lax.rem(mine + d, 4) * share + b * size

        @pl.loop(0, size)
        def _(t):
            k = jnp.minimum(first + t, pairs - 1)
            out_ref[b * size + t] = lax.dot_general(
                rows_ref[slot_ref[2 * k]],
                rows_ref[slot_ref[2 * k + 1]],
                (((1,), (1,)), ((), ())),
                preferred_element_type=jnp.float32,
            ).astype(out_ref.dtype)

    sums = {}
    for b in range(SUMMED_IN_PARTS):
        for d in (2, 1, 3):
            couplings(d, b, part_ref.at[d - 1])
            n = b * 3 + d - 1
            sums[b, d] = pltpu.make_async_remote_copy(
                src_ref=part_ref.at[d - 1, pl.ds(b * size, size)],
                dst_ref=inbox_ref.at[d - 1, pl.ds(b * size, size)],
                send_sem=sum_send.at[n],
                recv_sem=sum_recv.at[n],
                device_id=plane(d),
                device_id_type=MESH,
            )
            sums[b, d].start()
    for b in range(SUMMED_IN_PARTS):
        couplings(0, b, own_ref)

    row_id = lax.broadcasted_iota(jnp.int32, (width, width), 0)
    col_id = lax.broadcasted_iota(jnp.int32, (width, width), 1)

    def weigh(t):
        k = jnp.minimum(mine * share + t, pairs - 1)
        others = [inbox_ref[n, t].astype(jnp.float32) for n in range(3)]
        coupling = (own_ref[t] + others[0]) + (others[1] + others[2])
        by_col = jnp.broadcast_to(energy_in_ref[pl.ds(k, 1), :], (width, width))
        denom = by_col.T + by_col - fock_ref[occ_ref[2 * k]] - fock_ref[occ_ref[2 * k + 1]]
        inside = (row_id < count_ref[k]) & (col_id < count_ref[k])
        amplitude = jnp.where(inside, -coupling / denom, 0.0)
        mixed = 2.0 * amplitude - amplitude.T
        energy_ref[mine, pl.ds(t, 1), :] = jnp.sum(coupling * mixed, axis=0, keepdims=True)
        weights_ref[mine, t] = mixed.astype(jnp.bfloat16)

    copies = []

    def tell(ref, send, recv, n, d):
        copies.append(
            pltpu.make_async_remote_copy(
                src_ref=ref,
                dst_ref=ref,
                send_sem=send.at[n],
                recv_sem=recv.at[n],
                device_id=plane(d),
                device_id_type=MESH,
            )
        )
        copies[-1].start()

    for b in range(SUMMED_IN_PARTS):
        for d in (2, 1, 3):
            sums[b, d].wait_recv()
        pl.loop(b * size, (b + 1) * size)(weigh)
        for d in (2, 1, 3):
            tell(weights_ref.at[mine, pl.ds(b * size, size)], weight_send, weight_recv, b * 3 + d - 1, d)
    for d in (2, 1, 3):
        tell(energy_ref.at[mine], energy_send, energy_recv, d - 1, d)
    for copy in copies:
        copy.wait()
    for copy in sums.values():
        copy.wait_send()

    def produce(way, d, group):
        @pl.loop(0, 8)
        def _(t):
            slot = slot_at(way, group, t)
            pair = pair_ref[slot]
            weights = weights_ref[pair // share, lax.rem(pair, share)].astype(jnp.float32)
            weights = jnp.where(side_ref[slot] == 0, weights, weights.T).astype(jnp.bfloat16)
            send_ref[way, group, t] = jnp.dot(
                weights, rows_ref[partner_ref[slot]], preferred_element_type=jnp.float32
            ).astype(send_ref.dtype)

    exchange_in_kernel(
        produce, lambda way, group, t: recv_ref.at[way, group, t], OWN_FIRST, *exchange
    )


def pairs_kernel(
    half_ref, slot_ref, pair_ref, side_ref, partner_ref, occ_ref, count_ref, fock_ref, request_ref, energy_in_ref,
    coef_hbm_ref, ints_hbm_ref,
    gamma_ref, coef_ref, wanted_ref, energy_ref,
    rows_ref, *scratch,
):
    fetch, couple, (send_ref, transit_rows, transit_gamma), sems = scratch[:19], scratch[19:29], scratch[29:32], scratch[32:]
    fetch_rows(
        half_ref, request_ref, coef_hbm_ref, ints_hbm_ref, rows_ref, coef_ref, wanted_ref, *fetch,
        send_ref, transit_rows, *sems[:4],
    )
    couple_and_weigh(
        slot_ref, pair_ref, side_ref, partner_ref, occ_ref, count_ref, fock_ref, energy_in_ref, rows_ref,
        gamma_ref, energy_ref, *couple,
        send_ref, transit_gamma, *sems[4:],
    )


def grad_kernel(wanted_ref, coef_ref, gamma_ref, out_ref):
    step = pl.program_id(0)

    @pl.when(step == 0)
    def _():
        out_ref[...] = jnp.zeros_like(out_ref)

    for t in range(8):
        wanted = wanted_ref[slot_at_step(step, t)]
        coef = coef_ref[:, 0, 0, t].reshape(-1, coef_ref.shape[-1])
        coef = jnp.where(wanted > 0, coef, jnp.zeros_like(coef))
        term = jnp.dot(coef, gamma_ref[0, 0, t], preferred_element_type=jnp.float32).astype(jnp.bfloat16)
        out_ref[jnp.maximum(wanted - 1, 0)] += term.astype(jnp.float32)


def slot_at_step(step, t):
    group = lax.rem(step, 4)
    return jnp.where(step < 4, slot_at(0, group, t), slot_at(1, group, t))


def params(limit, collective_id=None):
    return pltpu.CompilerParams(
        vmem_limit_bytes=limit << 20, collective_id=collective_id, has_side_effects=collective_id is not None
    )


def local(three_index, fock_diag, pair_occ, pno_count, pno_energy, pno_coef):
    groups = lax.axis_size("pair")
    planes = lax.axis_size("aux")
    occ_dev, width_dom, width_aux = three_index.shape
    pair_dev = pair_occ.shape[0]
    width_pno = pno_coef.shape[3]
    halves = 2 * pair_dev
    slots = groups * CAPACITY
    part = width_dom // planes
    smem = pl.BlockSpec(memory_space=pltpu.SMEM)
    vmem = pl.BlockSpec(memory_space=pltpu.VMEM)
    hbm = pl.BlockSpec(memory_space=pl.ANY)

    slot_of, half_of, request, partner = plan_slots(pair_occ, groups, occ_dev)

    half = jnp.maximum(half_of, 0)
    coef_block = (part, width_pno)
    share = -(-pair_dev // planes)
    row_block = exchange_scratch((width_pno, width_aux))
    gamma, coef, wanted, energy_cols = pl.pallas_call(
        pairs_kernel,
        name="pairs",
        out_shape=(
            jax.ShapeDtypeStruct((CAPACITY, 4, 8, width_pno, width_aux), jnp.bfloat16),
            jax.ShapeDtypeStruct((planes, CAPACITY, 4, 8, part, width_pno), jnp.bfloat16),
            jax.ShapeDtypeStruct((slots,), jnp.int32),
            jax.ShapeDtypeStruct((planes, share, width_pno), jnp.float32),
        ),
        in_specs=[smem] * 8 + [vmem] * 2 + [hbm] * 2,
        out_specs=(hbm, vmem, smem, vmem),
        scratch_shapes=[
            pltpu.VMEM((slots, width_pno, width_aux), jnp.bfloat16),
            pltpu.VMEM((halves, part, width_pno), jnp.bfloat16),
            pltpu.SemaphoreType.DMA,
            pltpu.VMEM((occ_dev, width_dom, width_aux), jnp.bfloat16),
            pltpu.SemaphoreType.DMA,
            pltpu.VMEM((8, 4, 8, 128), jnp.int32),
            pltpu.SMEM((8, 4, 8, 128), jnp.int32),
            pltpu.SemaphoreType.DMA,
            pltpu.SemaphoreType.DMA((3,)),
            pltpu.SemaphoreType.DMA((3,)),
            pltpu.SemaphoreType.DMA((8,)),
            pltpu.SemaphoreType.DMA((8,)),
        ]
        + exchange_scratch(coef_block)
        + [pltpu.SemaphoreType.DMA((32,)), pltpu.SemaphoreType.DMA((32,))]
        + [
            pltpu.VMEM((share, width_pno, width_pno), jnp.float32),
            pltpu.VMEM((planes - 1, share, width_pno, width_pno), jnp.bfloat16),
            pltpu.VMEM((planes - 1, share, width_pno, width_pno), jnp.bfloat16),
            pltpu.VMEM((planes, share, width_pno, width_pno), jnp.bfloat16),
        ]
        + [pltpu.SemaphoreType.DMA((SUMMED_IN_PARTS * (planes - 1),))] * 4
        + [pltpu.SemaphoreType.DMA((planes - 1,))] * 2
        + row_block[:1]
        + row_block[1:2] * 2
        + row_block[2:] * 2,
        compiler_params=params(56, 1),
    )(
        half, slot_of, half // 2, half % 2, partner, pair_occ.reshape(halves), pno_count, fock_diag,
        jnp.pad(request[None, :], ((0, 7), (0, 128 - slots))), pno_energy,
        pltpu.with_memory_space_constraint(pno_coef.reshape(halves, width_dom, width_pno), pltpu.HBM),
        pltpu.with_memory_space_constraint(three_index, pltpu.HBM),
    )
    energy = jnp.sum(energy_cols, axis=2).reshape(-1)[:pair_dev] / (width_pno * width_pno)
    grad = pl.pallas_call(
        grad_kernel,
        name="add_terms",
        out_shape=jax.ShapeDtypeStruct((occ_dev, width_dom, width_aux), jnp.float32),
        grid_spec=pltpu.PrefetchScalarGridSpec(
            num_scalar_prefetch=1,
            grid=(8,),
            in_specs=[
                pl.BlockSpec((planes, 1, 1, 8, part, width_pno), lambda s, w: (0, s // 4, s % 4, 0, 0, 0)),
                pl.BlockSpec((1, 1, 8, width_pno, width_aux), lambda s, w: (s // 4, s % 4, 0, 0, 0)),
            ],
            out_specs=pl.BlockSpec((occ_dev, width_dom, width_aux), lambda s, w: (0, 0, 0)),
        ),
        compiler_params=params(49),
    )(wanted, *(pltpu.with_memory_space_constraint(x, pltpu.HBM) for x in (coef, gamma)))
    return energy, grad


def solution(mesh):
    placed = (
        P("pair", None, "aux"),
        P(),
        P("pair", None),
        P("pair"),
        P("pair", None),
        P("pair", None, None, None),
    )
    return jax.shard_map(
        local,
        mesh=mesh,
        in_specs=placed,
        out_specs=(P("pair"), P("pair", None, "aux")),
        check_vma=False,
    )
```
